32 devices in a mesh: grp: 2 (over x), chan: 8 (over z, y), tm: 2 (over core).
Axes of the slice: x: 2, y: 2, z: 4, core: 2. Of those that a mesh axis runs over, the one named last changes fastest.
Arguments:
- spectra: bfloat16 [1024, 32, 2, 128], P(('grp', 'chan'), 'tm'), parts along dimension 0, may hold values from -6 to 6
- channel_mask: int32 [1024], P(('grp', 'chan')), parts along dimension 0, may hold values 0 or 1
- window_mask: int32 [64], P(('grp', 'tm')), parts along dimension 0, may hold values 0 or 1
- source_block: int32 [4], replicated, may hold values from 0 to 7
Outputs:
- stacks: bfloat16 [4, 64, 1024, 128], P(None, 'tm', ('grp', 'chan')), parts along dimension 2
The draws below stay inside these ranges and needn't reach their ends.
There are 2 independent parts, one for each index of `grp`. The reference program is written for one: setup_inputs(seed, part) draws one part's arguments, and reference() takes and returns one part's arrays. A program takes and returns all parts, laid end to end along the dimension named above; an argument that names none is the same for every part. Nothing has to cross between parts.
All inputs are finite; a program needn't handle non-finite values. No bound on the sum of `channel_mask` or of `window_mask` on one device may be relied on, other than what follows from the above.
Results may differ from the reference program's by a relative error of at most 0.0075.
Values may be sent and summed in bfloat16 or wider, within the bound.
No kernel may reach another device: no remote copies, remote signals or barrier semaphores. Data moves between devices by JAX's collectives and lax.ppermute only.
A program may use at most 64 MiB of HBM per device.

```python
import math
import jax
import jax.numpy as jnp
from jax import lax

CH_DEV = 64
WIN_DEV = 16
F = 128
LAGS = 128
NFFT = 8192
LOW_BIN = 8
LAG_STEP = 28
STEPS = 4
CHANNELS = 512
WINDOWS = 32
N_CHAN = 8
N_TM = 2


def set_ends(entries, own_key, low, top_value):
    extent = entries.shape
    index_at = [jax.random.randint(jax.random.fold_in(own_key, axis), (), 0, extent[axis]) for axis in range(len(extent))]
    entries = entries.at[tuple(index_at)].set(low)
    longest = extent.index(max(extent))
    index_at[longest] = (index_at[longest] + 1) % extent[longest]
    return entries.at[tuple(index_at)].set(top_value)


def shard_levels(key, extent, shards, least, top_value):
    loudness = 1.0
    for dim, parts in shards:
        heights = jax.random.uniform(jax.random.fold_in(jax.random.fold_in(key, 6), dim), (parts,), jnp.float32, least / len(shards), top_value / len(shards))
        loudness = loudness * jnp.repeat(jnp.exp(heights), extent[dim] // parts).reshape((-1,) + (1,) * (len(extent) - 1 - dim))
    return loudness


def gaussian(rng, shape, deviation, limit, split=(), kind=jnp.bfloat16):
    loudness = shard_levels(rng, shape, split, -0.22, 0.18) if split else 1.0
    result = jax.random.normal(rng, shape, jnp.float32) * deviation * loudness
    return jnp.minimum(jnp.maximum(result, -limit), limit).astype(kind)


def setup_inputs(seed: int = 0, part: int = 0) -> dict:
    arg_keys = jax.random.split(jax.random.key(seed), 5)
    part_keys = jax.random.split(jax.random.fold_in(arg_keys[4], part), 5)
    return {
        "spectra": gaussian(part_keys[0], (CHANNELS, WINDOWS, 2, F), 1.0, 6.0, ((0, 8), (1, 2))),
        "channel_mask": set_ends((jax.random.randint(part_keys[1], (CHANNELS,), 0, 8) < 7).astype(jnp.int32), jax.random.fold_in(part_keys[1], 1), 0, 1),
        "window_mask": set_ends((jax.random.randint(part_keys[2], (WINDOWS,), 0, 4) < 3).astype(jnp.int32), jax.random.fold_in(part_keys[2], 1), 0, 1),
        "source_block": set_ends(jax.random.randint(arg_keys[3], (STEPS,), 0, N_CHAN), jax.random.fold_in(arg_keys[3], 1), 0, N_CHAN - 1).astype(jnp.int32),
    }


water_level = 0.1

def whiten(spectra, channel_mask, window_mask):
    values = spectra.astype(jnp.float32)
    magnitude = jnp.sqrt(values[:, :, 0] ** 2 + values[:, :, 1] ** 2)
    width = magnitude.shape[2]
    padded = jnp.pad(magnitude, ((0, 0), (0, 0), (2, 2)), mode='edge')
    smoothed = (padded[:, :, 0:width] + padded[:, :, 1:width + 1] + padded[:, :, 2:width + 2] + padded[:, :, 3:width + 3] + padded[:, :, 4:width + 4]) / 5.0
    keep_mask = channel_mask.astype(jnp.float32)[:, None] * window_mask.astype(jnp.float32)[None, :]
    scaling = keep_mask[:, :, None] / (smoothed + water_level)
    return (values * scaling[:, :, None, :]).astype(jnp.bfloat16)

def lag_tables(total_windows, bins):
    freq_index = jnp.arange(bins, dtype=jnp.int32) + LOW_BIN
    lag_index = (jnp.arange(LAGS, dtype=jnp.int32) - LAGS // 2) * LAG_STEP
    phase_index = freq_index[:, None] * lag_index[None, :] % NFFT
    phase = phase_index.astype(jnp.float32) * (2.0 * math.pi / NFFT)
    factor = 1.0 / math.sqrt(total_windows * bins)
    return (jnp.cos(phase) * factor, jnp.sin(phase) * factor)

def cross_lags(sources, receivers, flipped, cos_table, sin_table):
    real_part = jnp.einsum('swcf,rwcf->srf', sources.astype(jnp.float32), receivers.astype(jnp.float32), precision=lax.Precision.HIGHEST)
    imag_part = jnp.einsum('swcf,rwcf->srf', sources.astype(jnp.float32), flipped.astype(jnp.float32), precision=lax.Precision.HIGHEST)
    count_src = real_part.shape[0]
    count_rcv = real_part.shape[1]
    bins = real_part.shape[2]
    lagged = jnp.dot(real_part.reshape(count_src * count_rcv, bins), cos_table, precision=lax.Precision.HIGHEST) - jnp.dot(imag_part.reshape(count_src * count_rcv, bins), sin_table, precision=lax.Precision.HIGHEST)
    return lagged.reshape(count_src, count_rcv, cos_table.shape[1])

def reference(spectra, channel_mask, window_mask, source_block):
    whitened = whiten(spectra, channel_mask, window_mask)
    flipped = jnp.stack((whitened[:, :, 1], -whitened[:, :, 0]), axis=2)
    cos_table, sin_table = lag_tables(WINDOWS, F)
    blocks_rcv = whitened.reshape(N_CHAN, CH_DEV, WINDOWS, 2, F)
    blocks_flip = flipped.reshape(N_CHAN, CH_DEV, WINDOWS, 2, F)
    results = []
    for index in range(STEPS):
        first = (source_block[index] * CH_DEV).astype(jnp.int32)
        sources = lax.dynamic_slice_in_dim(whitened, first, CH_DEV, 0)

        def one_block(pair, sources=sources):
            receivers, turned = pair
            total = jnp.zeros((CH_DEV, CH_DEV, LAGS), jnp.float32)
            for half in range(N_TM):
                lowest = half * WIN_DEV
                partial_lags = cross_lags(sources[:, lowest:lowest + WIN_DEV], receivers[:, lowest:lowest + WIN_DEV], turned[:, lowest:lowest + WIN_DEV], cos_table, sin_table)
                rounded = lax.optimization_barrier(partial_lags.astype(jnp.bfloat16))
                total = total + rounded.astype(jnp.float32)
            return total.astype(jnp.bfloat16)
        stacked = lax.map(one_block, (blocks_rcv, blocks_flip))
        results.append(jnp.transpose(stacked, (1, 0, 2, 3)).reshape(CH_DEV, CHANNELS, LAGS))
    return jnp.stack(results)
```

```python
import functools
import math

import jax
import jax.numpy as jnp
import numpy as np
from jax import lax
from jax.experimental import pallas as pl
from jax.experimental.pallas import tpu as pltpu
from jax.sharding import PartitionSpec as P

LAGS = 128
NFFT = 8192
LOW_BIN = 8
LAG_STEP = 28
WATER = 0.1
BINS_TILE = 16

VMEM = pltpu.VMEM
SMEM = pltpu.SMEM


def ring_order(mesh):
    count = mesh.shape["chan"]
    natural = list(range(count))
    folded = natural[0::2] + natural[1::2][::-1]
    if count % 2:
        return natural
    grid = np.moveaxis(mesh.devices, mesh.axis_names.index("chan"), 0).reshape(count, -1)[:, 0]
    places = [getattr(device, "coords", None) for device in grid]
    if any(place is None for place in places):
        return folded if count == 8 else natural

    def length(tour):
        return sum(
            sum(abs(a - b) for a, b in zip(places[tour[i]], places[tour[i - 1]]))
            for i in range(count)
        )

    return folded if length(folded) < length(natural) else natural


def lag_tables(windows, bins):
    freq = np.arange(bins) + LOW_BIN
    lag = (np.arange(LAGS) - LAGS // 2) * LAG_STEP
    phase = (freq[:, None] * lag[None, :] % NFFT) * (2.0 * math.pi / NFFT)
    table = np.concatenate((np.cos(phase), -np.sin(phase))) / math.sqrt(windows * bins)
    return jnp.asarray(table, jnp.float32).astype(jnp.bfloat16)


def whiten_kernel(chan_mask, win_mask, spectra, same, other):
    rows, bins = spectra.shape[1:]
    half = same.shape[0]
    mine = lax.axis_index("tm") * half
    theirs = half - mine
    lane = lax.broadcasted_iota(jnp.int32, (rows, bins), 1)
    row = lax.broadcasted_iota(jnp.int32, (rows, bins), 0)
    even = row % 2 == 0
    keep = jnp.zeros((rows, bins), jnp.float32)
    for w in range(rows // 2):
        keep = jnp.where(row // 2 == w, win_mask[w].astype(jnp.float32), keep)

    def earlier(m):
        return jnp.where(lane == 0, m, pltpu.roll(m, 1, 1))

    def later(m):
        return jnp.where(lane == bins - 1, m, pltpu.roll(m, bins - 1, 1))

    def whitened(channel):
        values = spectra[channel].astype(jnp.float32)
        square = values * values
        pair = jnp.where(even, pltpu.roll(square, rows - 1, 0), pltpu.roll(square, 1, 0))
        magnitude = jnp.sqrt(square + pair)
        e1 = earlier(magnitude)
        l1 = later(magnitude)
        smoothed = (earlier(e1) + e1 + magnitude + l1 + later(l1)) / 5.0
        scaling = keep * chan_mask[channel].astype(jnp.float32) / (smoothed + WATER)
        return (values * scaling).astype(jnp.bfloat16)

    def step(i, _):
        same[i] = whitened(mine + i)
        other[i] = whitened(theirs + i)
        return 0

    lax.fori_loop(0, half, step, 0, unroll=4)


def whiten(spectra, chan_mask, win_mask):
    channels, rows, bins = spectra.shape
    piece = jax.ShapeDtypeStruct((channels // 2, rows, bins), jnp.bfloat16)
    return pl.pallas_call(
        whiten_kernel,
        out_shape=(piece, piece),
        in_specs=[
            pl.BlockSpec(memory_space=SMEM),
            pl.BlockSpec(memory_space=SMEM),
            pl.BlockSpec(memory_space=VMEM),
        ],
        out_specs=(pl.BlockSpec(memory_space=VMEM),) * 2,
        name="whiten",
    )(chan_mask, win_mask, spectra)


def stack_kernel(
    blocks, first, ids, steps, weights, table, *refs
):
    pieces = refs[: 2 * blocks]
    out = refs[2 * blocks + (0 if first else 1)]
    src, turned, cross, done, in_sem, out_sem = refs[2 * blocks + (1 if first else 2) :]
    sources, rows, bins = src.shape[1:]
    count = steps.shape[0]
    lanes = 2 * rows
    groups = bins // BINS_TILE
    per_tile = 128 // lanes
    tiles = BINS_TILE // per_tile
    row = lax.broadcasted_iota(jnp.int32, (BINS_TILE, 128), 0)
    col = lax.broadcasted_iota(jnp.int32, (BINS_TILE, 128), 1)
    receivers = weights.shape[1] // 2

    for block in range(blocks):
        matches = [steps[k] == ids[block] for k in range(count)]
        needed = functools.reduce(jnp.logical_or, matches)

        @pl.when(needed)
        def _(block=block):
            copies = [
                pltpu.make_async_copy(pieces[2 * block + h], src.at[h], in_sem.at[h]) for h in range(2)
            ]
            for copy in copies:
                copy.start()
            for copy in copies:
                copy.wait()

            def turn(s, _):
                a = jnp.concatenate([src[0, s], src[1, s]] * per_tile, axis=0)
                turned[s] = a.T
                return 0

            lax.fori_loop(0, sources, turn, 0, unroll=4)

            def products(g, _):
                b = turned[:, pl.ds(pl.multiple_of(g * BINS_TILE, BINS_TILE), BINS_TILE), :]
                wide = jnp.concatenate(
                    [
                        jnp.where(
                            (row == q * per_tile + col // lanes)[None], b, jnp.zeros_like(b)
                        ).reshape(sources * BINS_TILE, 128)
                        for q in range(tiles)
                    ],
                    axis=1,
                )
                depth = BINS_TILE * lanes
                x = jnp.dot(
                    wide,
                    weights[pl.ds(pl.multiple_of(g * depth, depth), depth), :],
                    preferred_element_type=jnp.float32,
                )
                cross[:, pl.ds(pl.multiple_of(g * BINS_TILE, BINS_TILE), BINS_TILE), :] = x.reshape(
                    sources, BINS_TILE, 2 * receivers
                ).astype(jnp.bfloat16)
                return 0

            lax.fori_loop(0, groups, products, 0)

            def lags(s, _):
                xs = [cross[s * 4 + i].T for i in range(4)]
                lhs = jnp.concatenate(
                    [jnp.concatenate([x[:receivers], x[receivers:]], axis=1) for x in xs], axis=0
                )
                y = jnp.dot(lhs, table[...], preferred_element_type=jnp.float32)
                done[pl.ds(s * 4, 4)] = y.reshape(4, receivers, LAGS).astype(jnp.bfloat16)
                return 0

            lax.fori_loop(0, sources // 4, lags, 0)

            for k in range(count):
                @pl.when(steps[k] == ids[block])
                def _(k=k):
                    pltpu.make_async_copy(done, out.at[k], out_sem.at[k]).start()
            for k in range(count):
                @pl.when(steps[k] == ids[block])
                def _(k=k):
                    pltpu.make_async_copy(done, out.at[k], out_sem.at[k]).wait()


def stack(ids, steps, weights, table, pieces, previous, out_shape):
    blocks = len(pieces) // 2
    sources, rows, bins = pieces[0].shape
    receivers = weights.shape[1] // 2
    first = previous is None
    args = [ids, steps, weights, table, *pieces] + ([] if first else [previous])
    return pl.pallas_call(
        functools.partial(stack_kernel, blocks, first),
        out_shape=out_shape,
        in_specs=[
            pl.BlockSpec(memory_space=SMEM),
            pl.BlockSpec(memory_space=SMEM),
            pl.BlockSpec(memory_space=VMEM),
            pl.BlockSpec(memory_space=VMEM),
        ]
        + [pl.BlockSpec(memory_space=pl.ANY)] * (len(args) - 4),
        out_specs=pl.BlockSpec(memory_space=pl.ANY),
        scratch_shapes=[
            VMEM((2, sources, rows, bins), jnp.bfloat16),
            VMEM((sources, bins, 128), jnp.bfloat16),
            VMEM((sources, bins, 2 * receivers), jnp.bfloat16),
            VMEM((sources, receivers, LAGS), jnp.bfloat16),
            pltpu.SemaphoreType.DMA((2,)),
            pltpu.SemaphoreType.DMA((steps.shape[0],)),
        ],
        input_output_aliases={} if first else {len(args) - 1: 0},
        compiler_params=pltpu.CompilerParams(vmem_limit_bytes=40 << 20),
        name="stack",
    )(*args)


def receiver_weights(same, other, far_same, far_other):
    low = jnp.concatenate((same, far_other), axis=1)
    high = jnp.concatenate((other, far_same), axis=1)
    second = lax.axis_index("tm") == 1
    rcv = jnp.where(second, jnp.concatenate((high, low)), jnp.concatenate((low, high)))
    channels, rows, bins = rcv.shape
    pairs = rcv.reshape(channels, rows // 2, 2, bins)
    turned = jnp.stack((pairs[:, :, 1], -pairs[:, :, 0]), axis=2).reshape(rcv.shape)
    both = jnp.stack((rcv, turned))
    return jnp.transpose(both, (3, 2, 0, 1)).reshape(bins * rows, 2 * channels)


def shards(ring, spectra, channel_mask, window_mask, source_block):
    count = len(ring)
    channels, windows, parts, bins = spectra.shape
    steps = source_block.shape[0]
    halves = lax.axis_size("tm")
    same, other = whiten(
        spectra.reshape(channels, windows * parts, bins), channel_mask, window_mask
    )

    def across(x):
        return lax.ppermute(x, "tm", [(0, 1), (1, 0)])

    def send(x, direction, cross=False):
        pairs = []
        for i in range(count):
            a, b = ring[i], ring[(i + direction) % count]
            for t in range(2):
                pairs.append((2 * a + t, 2 * b + (1 - t if cross else t)))
        return lax.ppermute(x, ("chan", "tm"), pairs)

    table = lag_tables(windows * halves, bins)
    place = np.zeros(count, np.int32)
    place[list(ring)] = np.arange(count)
    me = jnp.asarray(place)[lax.axis_index("chan")]
    tour = jnp.asarray(np.asarray(ring, np.int32))

    def owner(distance):
        return tour[(me + distance) % count]

    far_other = across(other)
    far_same = across(same)
    out_shape = jax.ShapeDtypeStruct((steps, channels // 2, channels, LAGS), jnp.bfloat16)
    run = functools.partial(stack, out_shape=out_shape)
    weights = receiver_weights(same, other, far_same, far_other)

    forward = (send(same, 1), send(other, 1, True))
    backward = (send(same, -1), send(other, -1, True))
    out = run(owner(0)[None], source_block, weights, table, (same, far_other), None)
    half = count // 2
    for hop in range(1, half):
        ids = jnp.stack((owner(-hop), owner(hop)))
        pieces = forward + backward
        if hop < half - 1:
            forward = tuple(send(x, 1) for x in forward)
            backward = tuple(send(x, -1) for x in backward)
        else:
            forward = (send(forward[0], 1),)
            backward = (send(backward[1], -1),)
        out = run(ids, source_block, weights, table, pieces, out)
    return run(owner(half)[None], source_block, weights, table, forward + backward, out)


def solution(mesh):
    placed = (P(("grp", "chan"), "tm", None, None), P(("grp", "chan")), P(("grp", "tm")), P())
    return jax.shard_map(
        functools.partial(shards, ring_order(mesh)),
        mesh=mesh,
        in_specs=placed,
        out_specs=P(None, "tm", ("grp", "chan"), None),
        check_vma=False,
    )
```

```python
import functools
import math

import jax
import jax.numpy as jnp
import numpy as np
from jax import lax
from jax.experimental import pallas as pl
from jax.experimental.pallas import tpu as pltpu
from jax.sharding import PartitionSpec as P

LAGS = 128
NFFT = 8192
LOW_BIN = 8
LAG_STEP = 28
WATER = 0.1
BINS_TILE = 16

VMEM = pltpu.VMEM
SMEM = pltpu.SMEM


def ring_order(mesh):
    count = mesh.shape["chan"]
    natural = list(range(count))
    folded = natural[0::2] + natural[1::2][::-1]
    if count % 2:
        return natural
    grid = np.moveaxis(mesh.devices, mesh.axis_names.index("chan"), 0).reshape(count, -1)[:, 0]
    places = [getattr(device, "coords", None) for device in grid]
    if any(place is None for place in places):
        return folded if count == 8 else natural

    def length(tour):
        return sum(
            sum(abs(a - b) for a, b in zip(places[tour[i]], places[tour[i - 1]]))
            for i in range(count)
        )

    return folded if length(folded) < length(natural) else natural


def lag_tables(windows, bins):
    freq = np.arange(bins) + LOW_BIN
    lag = (np.arange(LAGS) - LAGS // 2) * LAG_STEP
    phase = (freq[:, None] * lag[None, :] % NFFT) * (2.0 * math.pi / NFFT)
    table = np.concatenate((np.cos(phase), -np.sin(phase))) / math.sqrt(windows * bins)
    return jnp.asarray(table, jnp.float32).astype(jnp.bfloat16)


def whiten_kernel(chan_mask, win_mask, spectra, same, other):
    rows, bins = spectra.shape[1:]
    half = same.shape[0]
    mine = lax.axis_index("tm") * half
    theirs = half - mine
    lane = lax.broadcasted_iota(jnp.int32, (rows, bins), 1)
    row = lax.broadcasted_iota(jnp.int32, (rows, bins), 0)
    even = row % 2 == 0
    keep = jnp.zeros((rows, bins), jnp.float32)
    for w in range(rows // 2):
        keep = jnp.where(row // 2 == w, win_mask[w].astype(jnp.float32), keep)

    def earlier(m):
        return jnp.where(lane == 0, m, pltpu.roll(m, 1, 1))

    def later(m):
        return jnp.where(lane == bins - 1, m, pltpu.roll(m, bins - 1, 1))

    def whitened(channel):
        values = spectra[channel].astype(jnp.float32)
        square = values * values
        pair = jnp.where(even, pltpu.roll(square, rows - 1, 0), pltpu.roll(square, 1, 0))
        magnitude = jnp.sqrt(square + pair)
        e1 = earlier(magnitude)
        l1 = later(magnitude)
        smoothed = (earlier(e1) + e1 + magnitude + l1 + later(l1)) / 5.0
        scaling = keep * chan_mask[channel].astype(jnp.float32) / (smoothed + WATER)
        return (values * scaling).astype(jnp.bfloat16)

    def step(i, _):
        same[i] = whitened(mine + i)
        other[i] = whitened(theirs + i)
        return 0

    lax.fori_loop(0, half, step, 0, unroll=4)


def whiten(spectra, chan_mask, win_mask):
    channels, rows, bins = spectra.shape
    piece = jax.ShapeDtypeStruct((channels // 2, rows, bins), jnp.bfloat16)
    return pl.pallas_call(
        whiten_kernel,
        out_shape=(piece, piece),
        in_specs=[
            pl.BlockSpec(memory_space=SMEM),
            pl.BlockSpec(memory_space=SMEM),
            pl.BlockSpec(memory_space=VMEM),
        ],
        out_specs=(pl.BlockSpec(memory_space=VMEM),) * 2,
        name="whiten",
    )(chan_mask, win_mask, spectra)


def receiver_kernel(same, other, far_same, far_other, weights, flat, wide):
    half, rows, bins = same.shape
    mine = lax.axis_index("tm") * half
    theirs = half - mine
    deep = 2 * rows
    for i in range(half):
        for start, near, far in ((mine, same, far_other), (theirs, other, far_same)):
            at = pl.multiple_of((start + i) * deep, deep)
            flat[pl.ds(at, rows), :] = near[i].astype(jnp.float32)
            flat[pl.ds(at + rows, rows), :] = far[i].astype(jnp.float32)
    for w in range(rows):
        real = flat[pl.ds(2 * w, 2 * half, stride=deep), :]
        imag = flat[pl.ds(2 * w + 1, 2 * half, stride=deep), :]
        wide[pl.ds(2 * w, bins, stride=deep), :] = jnp.concatenate((real, imag)).T
        wide[pl.ds(2 * w + 1, bins, stride=deep), :] = jnp.concatenate((imag, -real)).T
    weights[...] = wide[...].astype(jnp.bfloat16)


def receiver_weights(same, other, far_same, far_other):
    half, rows, bins = same.shape
    return pl.pallas_call(
        receiver_kernel,
        out_shape=jax.ShapeDtypeStruct((bins * 2 * rows, 4 * half), jnp.bfloat16),
        in_specs=[pl.BlockSpec(memory_space=VMEM)] * 4,
        out_specs=pl.BlockSpec(memory_space=VMEM),
        scratch_shapes=[
            VMEM((2 * half * 2 * rows, bins), jnp.float32),
            VMEM((bins * 2 * rows, 4 * half), jnp.float32),
        ],
        compiler_params=pltpu.CompilerParams(vmem_limit_bytes=24 << 20),
        cost_estimate=pl.CostEstimate(flops=2 << 30, bytes_accessed=12 << 20, transcendentals=0),
        name="receiver_weights",
    )(same, other, far_same, far_other)


def stack_kernel(distances, first, tour, place, steps, weights, table, *refs):
    blocks = len(distances)
    pieces = refs[: 2 * blocks]
    out = refs[2 * blocks + (0 if first else 1)]
    src, turned, cross, done, in_sem, out_sem = refs[2 * blocks + (1 if first else 2) :]
    sources, rows, bins = src.shape[2:]
    count = steps.shape[0]
    ring = tour.shape[0]
    lanes = 2 * rows
    per_tile = 128 // lanes
    tiles = BINS_TILE // per_tile
    depth = BINS_TILE * lanes
    row = lax.broadcasted_iota(jnp.int32, (BINS_TILE, 128), 0)
    col = lax.broadcasted_iota(jnp.int32, (BINS_TILE, 128), 1)
    receivers = weights.shape[1] // 2
    me = place[lax.axis_index("chan")]
    owners = [tour[lax.rem(me + d + ring, ring)] for d in distances]
    needed = [
        functools.reduce(jnp.logical_or, [steps[k] == owner for k in range(count)])
        for owner in owners
    ]
    part = sources // 2

    def arrival(b, h):
        return pltpu.make_async_copy(pieces[2 * b + h], src.at[b, h], in_sem.at[b, h])

    for b in range(blocks):
        @pl.when(needed[b])
        def _(b=b):
            for h in range(2):
                arrival(b, h).start()

    def departure(b, k, c):
        return pltpu.make_async_copy(
            done.at[b, pl.ds(c * part, part)], out.at[k, pl.ds(c * part, part)], out_sem.at[b, k, c]
        )

    def compute(b, owner):
        for s in range(sources):
            turned[s] = jnp.concatenate([src[b, 0, s], src[b, 1, s]] * per_tile, axis=0).T
        for g in range(bins // BINS_TILE):
            at = g * BINS_TILE
            mine = turned[:, at : at + BINS_TILE, :]
            wide = jnp.concatenate(
                [
                    jnp.where(
                        (row == q * per_tile + col // lanes)[None], mine, jnp.zeros_like(mine)
                    ).reshape(sources * BINS_TILE, 128)
                    for q in range(tiles)
                ],
                axis=1,
            )
            x = jnp.dot(
                wide, weights[g * depth : (g + 1) * depth, :], preferred_element_type=jnp.float32
            )
            cross[:, at : at + BINS_TILE, :] = x.reshape(sources, BINS_TILE, 2 * receivers).astype(
                jnp.bfloat16
            )
        for c in range(2):
            turns = [cross[c * part + i].T for i in range(part)]
            left = jnp.concatenate(
                [jnp.concatenate([x[:receivers], x[receivers:]], axis=1) for x in turns]
            )
            y = jnp.dot(left, table[...], preferred_element_type=jnp.float32)
            done[b, c * part : (c + 1) * part] = y.reshape(part, receivers, LAGS).astype(
                jnp.bfloat16
            )
            for k in range(count):
                @pl.when(steps[k] == owner)
                def _(k=k, c=c):
                    departure(b, k, c).start()

    def turn(b, _):
        later = b == blocks - 1
        owner = jnp.where(later, owners[-1], owners[0])

        @pl.when(jnp.where(later, needed[-1], needed[0]))
        def _():
            for i in range(blocks):
                @pl.when(b == i)
                def _(i=i):
                    for h in range(2):
                        arrival(i, h).wait()
            compute(b, owner)
        return 0

    lax.fori_loop(0, blocks, turn, 0)
    for b in range(blocks):
        for k in range(count):
            @pl.when(steps[k] == owners[b])
            def _(b=b, k=k):
                for c in range(2):
                    departure(b, k, c).wait()


def stack(distances, tour, place, steps, weights, table, pieces, previous, out_shape):
    blocks = len(distances)
    sources, rows, bins = pieces[0].shape
    receivers = weights.shape[1] // 2
    count = steps.shape[0]
    first = previous is None
    args = [tour, place, steps, weights, table, *pieces] + ([] if first else [previous])
    return pl.pallas_call(
        functools.partial(stack_kernel, distances, first),
        out_shape=out_shape,
        in_specs=[pl.BlockSpec(memory_space=SMEM)] * 3
        + [pl.BlockSpec(memory_space=VMEM)] * 2
        + [pl.BlockSpec(memory_space=pl.ANY)] * (len(args) - 5),
        out_specs=pl.BlockSpec(memory_space=pl.ANY),
        scratch_shapes=[
            VMEM((blocks, 2, sources, rows, bins), jnp.bfloat16),
            VMEM((sources, bins, 128), jnp.bfloat16),
            VMEM((sources, bins, 2 * receivers), jnp.bfloat16),
            VMEM((blocks, sources, receivers, LAGS), jnp.bfloat16),
            pltpu.SemaphoreType.DMA((blocks, 2)),
            pltpu.SemaphoreType.DMA((blocks, count, 2)),
        ],
        input_output_aliases={} if first else {len(args) - 1: 0},
        compiler_params=pltpu.CompilerParams(vmem_limit_bytes=24 << 20),
        cost_estimate=pl.CostEstimate(
            flops=blocks * (3 << 30), bytes_accessed=blocks << 20, transcendentals=0
        ),
        name="stack",
    )(*args)


def shards(ring, spectra, channel_mask, window_mask, source_block):
    count = len(ring)
    channels, windows, parts, bins = spectra.shape
    steps = source_block.shape[0]
    halves = lax.axis_size("tm")
    same, other = whiten(
        spectra.reshape(channels, windows * parts, bins), channel_mask, window_mask
    )

    def across(x):
        return lax.ppermute(x, "tm", [(0, 1), (1, 0)])

    def send(x, direction, cross=False):
        pairs = []
        for i in range(count):
            a, b = ring[i], ring[(i + direction) % count]
            for t in range(2):
                pairs.append((2 * a + t, 2 * b + (1 - t if cross else t)))
        return lax.ppermute(x, ("chan", "tm"), pairs)

    table = lag_tables(windows * halves, bins)
    place = np.zeros(count, np.int32)
    place[list(ring)] = np.arange(count)
    where = (jnp.asarray(np.asarray(ring, np.int32)), jnp.asarray(place))

    forward = (send(same, 1), send(other, 1, True))
    backward = (send(same, -1), send(other, -1, True))
    far_other = across(other)
    far_same = across(same)
    weights = receiver_weights(same, other, far_same, far_other)
    run = functools.partial(
        stack,
        out_shape=jax.ShapeDtypeStruct((steps, channels // 2, channels, LAGS), jnp.bfloat16),
    )
    rest = (*where, source_block, weights, table)
    out = run((0,), *rest, (same, far_other), None)
    half = count // 2
    for hop in range(1, half):
        pieces = forward + backward
        if hop < half - 1:
            forward = tuple(send(x, 1) for x in forward)
            backward = tuple(send(x, -1) for x in backward)
        else:
            forward = (send(forward[0], 1),)
            backward = (send(backward[1], -1),)
        out = run((-hop, hop), *rest, pieces, out)
    return run((half,), *rest, forward + backward, out)


def solution(mesh):
    placed = (P(("grp", "chan"), "tm", None, None), P(("grp", "chan")), P(("grp", "tm")), P())
    return jax.shard_map(
        functools.partial(shards, ring_order(mesh)),
        mesh=mesh,
        in_specs=placed,
        out_specs=P(None, "tm", ("grp", "chan"), None),
        check_vma=False,
    )
```

```python
import functools
import math

import jax
import jax.numpy as jnp
import numpy as np
from jax import lax
from jax.experimental import pallas as pl
from jax.experimental.pallas import tpu as pltpu
from jax.sharding import PartitionSpec as P

LAGS = 128
NFFT = 8192
LOW_BIN = 8
LAG_STEP = 28
WATER = 0.1
BATCH = 8
GROUP = 8

VMEM = pltpu.VMEM
SMEM = pltpu.SMEM


def ring_order(mesh):
    count = mesh.shape["chan"]
    natural = list(range(count))
    folded = natural[0::2] + natural[1::2][::-1]
    if count % 2:
        return natural
    grid = np.moveaxis(mesh.devices, mesh.axis_names.index("chan"), 0).reshape(count, -1)[:, 0]
    places = [getattr(device, "coords", None) for device in grid]
    if any(place is None for place in places):
        return folded if count == 8 else natural

    def length(tour):
        return sum(
            sum(abs(a - b) for a, b in zip(places[tour[i]], places[tour[i - 1]]))
            for i in range(count)
        )

    return folded if length(folded) < length(natural) else natural


def lag_tables(windows, bins):
    freq = np.arange(bins) + LOW_BIN
    lag = (np.arange(LAGS) - LAGS // 2) * LAG_STEP
    phase = (freq[:, None] * lag[None, :] % NFFT) * (2.0 * math.pi / NFFT)
    table = np.concatenate((np.cos(phase), -np.sin(phase))) / math.sqrt(windows * bins)
    return jnp.asarray(table, jnp.float32).astype(jnp.bfloat16)


def interleave(first, second):
    bins = first.shape[-1]
    lane = lax.broadcasted_iota(jnp.int32, first.shape, 1)
    even = lane // GROUP % 2 == 0
    return (
        jnp.where(even, first, pltpu.roll(second, GROUP, 1)),
        jnp.where(even, pltpu.roll(first, bins - GROUP, 1), second),
    )


def whiten_kernel(chan_mask, win_mask, spectra, same, other):
    rows, bins = spectra.shape[1:]
    half = same.shape[0]
    mine = lax.axis_index("tm") * half
    theirs = half - mine
    row = lax.broadcasted_iota(jnp.int32, (rows, bins), 0)
    keep = jnp.zeros((rows, bins), jnp.float32)
    for w in range(rows // 2):
        keep = jnp.where(row // 2 == w, win_mask[w].astype(jnp.float32), keep)

    source = lax.broadcasted_iota(jnp.int32, (bins, bins), 0)
    target = lax.broadcasted_iota(jnp.int32, (bins, bins), 1)
    band = sum(
        jnp.where(source == jnp.clip(target + d, 0, bins - 1), 1.0, 0.0) for d in range(-2, 3)
    ).astype(jnp.bfloat16)
    band = jnp.concatenate([band] * 3)

    def with_partner(square):
        even = lax.broadcasted_iota(jnp.int32, square.shape, 0) % 2 == 0
        last = square.shape[0] - 1
        return square + jnp.where(even, pltpu.roll(square, last, 0), pltpu.roll(square, 1, 0))

    def whitened(channels):
        values = jnp.concatenate([spectra[c].astype(jnp.float32) for c in channels])
        square = values * values
        power = jnp.concatenate(
            [with_partner(square[i : i + 8]) for i in range(0, square.shape[0], 8)]
        )
        magnitude = jnp.sqrt(power)
        high = magnitude.astype(jnp.bfloat16)
        rest = magnitude - high.astype(jnp.float32)
        middle = rest.astype(jnp.bfloat16)
        low = (rest - middle.astype(jnp.float32)).astype(jnp.bfloat16)
        smoothed = (
            jnp.dot(
                jnp.concatenate((high, middle, low), axis=1),
                band,
                preferred_element_type=jnp.float32,
            )
            / 5.0
        )
        kept = jnp.concatenate([keep * chan_mask[c].astype(jnp.float32) for c in channels])
        return values * (kept / (smoothed + WATER))

    def step(i, _):
        for start, piece in ((mine, same), (theirs, other)):
            values = whitened([start + i * BATCH + j for j in range(BATCH)])
            for j in range(0, BATCH, 2):
                pair = interleave(
                    values[j * rows : (j + 1) * rows], values[(j + 1) * rows : (j + 2) * rows]
                )
                piece[i * BATCH + j] = pair[0].astype(jnp.bfloat16)
                piece[i * BATCH + j + 1] = pair[1].astype(jnp.bfloat16)
        return 0

    lax.fori_loop(0, half // BATCH, step, 0, unroll=2)


def whiten(spectra, chan_mask, win_mask):
    channels, rows, bins = spectra.shape
    piece = jax.ShapeDtypeStruct((channels // 2, rows, bins), jnp.bfloat16)
    return pl.pallas_call(
        whiten_kernel,
        out_shape=(piece, piece),
        in_specs=[
            pl.BlockSpec(memory_space=SMEM),
            pl.BlockSpec(memory_space=SMEM),
            pl.BlockSpec(memory_space=VMEM),
        ],
        out_specs=(pl.BlockSpec(memory_space=VMEM),) * 2,
        name="whiten",
    )(chan_mask, win_mask, spectra)


def receiver_kernel(same, other, far_same, far_other, weights, flat, wide):
    half, rows, bins = same.shape
    mine = lax.axis_index("tm") * half
    theirs = half - mine
    deep = 2 * rows
    for i in range(0, half, 2):
        for start, sides in ((mine, (same, far_other)), (theirs, (other, far_same))):
            for h, piece in enumerate(sides):
                pair = interleave(piece[i].astype(jnp.float32), piece[i + 1].astype(jnp.float32))
                for j in range(2):
                    at = pl.multiple_of((start + i + j) * deep + h * rows, rows)
                    flat[pl.ds(at, rows), :] = pair[j]
    for w in range(rows):
        real = flat[pl.ds(2 * w, 2 * half, stride=deep), :]
        imag = flat[pl.ds(2 * w + 1, 2 * half, stride=deep), :]
        wide[pl.ds(2 * w, bins, stride=deep), :] = jnp.concatenate((real, imag)).T
        wide[pl.ds(2 * w + 1, bins, stride=deep), :] = jnp.concatenate((imag, -real)).T
    weights[...] = wide[...].astype(jnp.bfloat16)


def receiver_weights(same, other, far_same, far_other):
    half, rows, bins = same.shape
    return pl.pallas_call(
        receiver_kernel,
        out_shape=jax.ShapeDtypeStruct((bins * 2 * rows, 4 * half), jnp.bfloat16),
        in_specs=[pl.BlockSpec(memory_space=VMEM)] * 4,
        out_specs=pl.BlockSpec(memory_space=VMEM),
        scratch_shapes=[
            VMEM((2 * half * 2 * rows, bins), jnp.float32),
            VMEM((bins * 2 * rows, 4 * half), jnp.float32),
        ],
        compiler_params=pltpu.CompilerParams(vmem_limit_bytes=24 << 20),
        cost_estimate=pl.CostEstimate(flops=2 << 30, bytes_accessed=12 << 20, transcendentals=0),
        name="receiver_weights",
    )(same, other, far_same, far_other)


def stack_kernel(distances, first, tour, place, steps, table, weights, *refs):
    blocks = len(distances)
    pieces = refs[: 2 * blocks]
    out = refs[2 * blocks + (0 if first else 1)]
    src, turned, cross, done, in_sem, out_sem = refs[2 * blocks + (1 if first else 2) :]
    sources, rows, bins = src.shape[2:]
    count = steps.shape[0]
    ring = tour.shape[0]
    lanes = 2 * rows
    per_tile = 128 // lanes
    tiles = GROUP // per_tile
    depth = GROUP * lanes
    pair_rows = 2 * GROUP
    row = lax.broadcasted_iota(jnp.int32, (pair_rows, 128), 0) % GROUP
    col = lax.broadcasted_iota(jnp.int32, (pair_rows, 128), 1) // lanes
    receivers = weights.shape[1] // 2
    me = place[lax.axis_index("chan")]
    owners = [tour[lax.rem(me + d + ring, ring)] for d in distances]
    needed = [
        functools.reduce(jnp.logical_or, [steps[k] == owner for k in range(count)])
        for owner in owners
    ]
    part = sources // 2

    def arrival(b, h):
        return pltpu.make_async_copy(pieces[2 * b + h], src.at[b, h], in_sem.at[b, h])

    for b in range(blocks):
        @pl.when(needed[b])
        def _(b=b):
            for h in range(2):
                arrival(b, h).start()

    def departure(b, k, c):
        return pltpu.make_async_copy(
            done.at[b, pl.ds(c * part, part)], out.at[k, pl.ds(c * part, part)], out_sem.at[b, k, c]
        )

    def compute(b, owner):
        for s in range(sources):
            turned[s // 2, s % 2] = jnp.concatenate([src[b, 0, s], src[b, 1, s]] * per_tile).T
        for m in range(bins // pair_rows):
            at = m * pair_rows
            sums = []
            for p in range(2):
                mine = turned[:, p, at : at + pair_rows, :]
                wide = jnp.concatenate(
                    [
                        jnp.where(
                            (row == q * per_tile + col)[None], mine, jnp.zeros_like(mine)
                        ).reshape(sources * GROUP, 128)
                        for q in range(tiles)
                    ],
                    axis=1,
                )
                start = (2 * m + p) * depth
                x = jnp.dot(
                    wide, weights[start : start + depth, :], preferred_element_type=jnp.float32
                )
                sums.append(x.reshape(sources, GROUP, 2 * receivers))
            cross[:, at : at + pair_rows, :] = jnp.concatenate(sums, axis=1).astype(jnp.bfloat16)
        for c in range(2):
            turns = [cross[c * part + i].T for i in range(part)]
            left = jnp.concatenate(
                [jnp.concatenate([x[:receivers], x[receivers:]], axis=1) for x in turns]
            )
            y = jnp.dot(left, table[...], preferred_element_type=jnp.float32)
            done[b, c * part : (c + 1) * part] = y.reshape(part, receivers, LAGS).astype(
                jnp.bfloat16
            )
            for k in range(count):
                @pl.when(steps[k] == owner)
                def _(k=k, c=c):
                    departure(b, k, c).start()

    def turn(b, _):
        later = b == blocks - 1
        owner = jnp.where(later, owners[-1], owners[0])

        @pl.when(jnp.where(later, needed[-1], needed[0]))
        def _():
            for i in range(blocks):
                @pl.when(b == i)
                def _(i=i):
                    for h in range(2):
                        arrival(i, h).wait()
            compute(b, owner)
        return 0

    lax.fori_loop(0, blocks, turn, 0)
    for b in range(blocks):
        for k in range(count):
            @pl.when(steps[k] == owners[b])
            def _(b=b, k=k):
                for c in range(2):
                    departure(b, k, c).wait()


def stack(distances, tour, place, steps, table, weights, pieces, previous, out_shape):
    blocks = len(distances)
    sources, rows, bins = pieces[0].shape
    receivers = weights.shape[1] // 2
    count = steps.shape[0]
    first = previous is None
    args = [tour, place, steps, table, weights, *pieces] + ([] if first else [previous])
    return pl.pallas_call(
        functools.partial(stack_kernel, distances, first),
        out_shape=out_shape,
        in_specs=[pl.BlockSpec(memory_space=SMEM)] * 3
        + [pl.BlockSpec(memory_space=VMEM)] * 2
        + [pl.BlockSpec(memory_space=pl.ANY)] * (len(args) - 5),
        out_specs=pl.BlockSpec(memory_space=pl.ANY),
        scratch_shapes=[
            VMEM((blocks, 2, sources, rows, bins), jnp.bfloat16),
            VMEM((sources // 2, 2, bins, 128), jnp.bfloat16),
            VMEM((sources, bins, 2 * receivers), jnp.bfloat16),
            VMEM((blocks, sources, receivers, LAGS), jnp.bfloat16),
            pltpu.SemaphoreType.DMA((blocks, 2)),
            pltpu.SemaphoreType.DMA((blocks, count, 2)),
        ],
        input_output_aliases={} if first else {len(args) - 1: 0},
        compiler_params=pltpu.CompilerParams(vmem_limit_bytes=24 << 20),
        cost_estimate=pl.CostEstimate(
            flops=blocks * (3 << 30), bytes_accessed=blocks << 20, transcendentals=0
        ),
        name="stack",
    )(*args)


def shards(ring, spectra, channel_mask, window_mask, source_block):
    count = len(ring)
    channels, windows, parts, bins = spectra.shape
    steps = source_block.shape[0]
    halves = lax.axis_size("tm")
    same, other = whiten(
        spectra.reshape(channels, windows * parts, bins), channel_mask, window_mask
    )

    def across(x):
        return lax.ppermute(x, "tm", [(0, 1), (1, 0)])

    def send(x, direction, cross=False):
        pairs = []
        for i in range(count):
            a, b = ring[i], ring[(i + direction) % count]
            for t in range(2):
                pairs.append((2 * a + t, 2 * b + (1 - t if cross else t)))
        return lax.ppermute(x, ("chan", "tm"), pairs)

    table = lag_tables(windows * halves, bins)
    place = np.zeros(count, np.int32)
    place[list(ring)] = np.arange(count)
    where = (jnp.asarray(np.asarray(ring, np.int32)), jnp.asarray(place))

    half = count // 2
    tie = lax.optimization_barrier
    early = (send(same, 1), send(same, -1))
    far_same = across(same)
    far_other = across(other)
    late = (send(other, 1, True), send(other, -1, True))
    weights = receiver_weights(same, other, far_same, far_other)
    run = functools.partial(
        stack,
        out_shape=jax.ShapeDtypeStruct((steps, channels // 2, channels, LAGS), jnp.bfloat16),
    )
    rest = (*where, source_block, table)
    out = held = None
    for hop in range(1, half):
        closing = hop == half - 1
        if hop == 1:
            early, weights = tie((early, weights))
        else:
            early, out = tie((early, out))
        coming = (send(early[0], 1), None if closing else send(early[1], -1))
        if hop > 1:
            out = run((1 - hop, hop - 1), *rest, weights, held, out)
            late, out = tie((late, out))
        else:
            late, weights = tie((late, weights))
        held = (early[0], late[0], early[1], late[1])
        later = (None if closing else send(late[0], 1), send(late[1], -1))
        if hop == 1:
            out = run((0,), *rest, weights, (same, far_other), None)
        early, late = coming, later
    out = run((1 - half, half - 1), *rest, weights, held, out)
    return run((half,), *rest, weights, (early[0], late[1]), out)


def solution(mesh):
    placed = (P(("grp", "chan"), "tm", None, None), P(("grp", "chan")), P(("grp", "tm")), P())
    return jax.shard_map(
        functools.partial(shards, ring_order(mesh)),
        mesh=mesh,
        in_specs=placed,
        out_specs=P(None, "tm", ("grp", "chan"), None),
        check_vma=False,
    )
```

```python
import functools
import math

import jax
import jax.numpy as jnp
import numpy as np
from jax import lax
from jax.experimental import pallas as pl
from jax.experimental.pallas import tpu as pltpu
from jax.sharding import PartitionSpec as P

LAGS = 128
NFFT = 8192
LOW_BIN = 8
LAG_STEP = 28
WATER = 0.1
BATCH = 8
GROUP = 8

VMEM = pltpu.VMEM
SMEM = pltpu.SMEM
SMALL = pl.CostEstimate(flops=1 << 20, bytes_accessed=1 << 14, transcendentals=0)


def ring_order(mesh):
    count = mesh.shape["chan"]
    natural = list(range(count))
    folded = natural[0::2] + natural[1::2][::-1]
    if count % 2:
        return natural
    grid = np.moveaxis(mesh.devices, mesh.axis_names.index("chan"), 0).reshape(count, -1)[:, 0]
    places = [getattr(device, "coords", None) for device in grid]
    if any(place is None for place in places):
        return folded if count == 8 else natural

    def length(tour):
        return sum(
            sum(abs(a - b) for a, b in zip(places[tour[i]], places[tour[i - 1]]))
            for i in range(count)
        )

    return folded if length(folded) < length(natural) else natural


def lag_tables(windows, bins):
    freq = np.arange(bins) + LOW_BIN
    lag = (np.arange(LAGS) - LAGS // 2) * LAG_STEP
    phase = (freq[:, None] * lag[None, :] % NFFT) * (2.0 * math.pi / NFFT)
    table = np.concatenate((np.cos(phase), -np.sin(phase))) / math.sqrt(windows * bins)
    return jnp.asarray(table, jnp.float32).astype(jnp.bfloat16)


def interleave(first, second):
    bins = first.shape[-1]
    lane = lax.broadcasted_iota(jnp.int32, first.shape, 1)
    even = lane // GROUP % 2 == 0
    return (
        jnp.where(even, first, pltpu.roll(second, GROUP, 1)),
        jnp.where(even, pltpu.roll(first, bins - GROUP, 1), second),
    )


def whiten_kernel(chan_mask, win_mask, spectra, same, other, held, sems):
    rows, bins = spectra.shape[1:]
    half = same.shape[0]
    own = lax.axis_index("tm") * half
    starts = (own, half - own)
    copies = [
        pltpu.make_async_copy(spectra.at[pl.ds(start, half)], held.at[i], sems.at[i])
        for i, start in enumerate(starts)
    ]
    for copy in copies:
        copy.start()
    row = lax.broadcasted_iota(jnp.int32, (rows, bins), 0)
    keep = jnp.zeros((rows, bins), jnp.float32)
    for w in range(rows // 2):
        keep = jnp.where(row // 2 == w, win_mask[w].astype(jnp.float32), keep)

    source = lax.broadcasted_iota(jnp.int32, (bins, bins), 0)
    target = lax.broadcasted_iota(jnp.int32, (bins, bins), 1)
    band = sum(
        jnp.where(source == jnp.clip(target + d, 0, bins - 1), 1.0, 0.0) for d in range(-2, 3)
    ).astype(jnp.bfloat16)
    band = jnp.concatenate([band] * 3)

    def with_partner(square):
        even = lax.broadcasted_iota(jnp.int32, square.shape, 0) % 2 == 0
        last = square.shape[0] - 1
        return square + jnp.where(even, pltpu.roll(square, last, 0), pltpu.roll(square, 1, 0))

    def whitened(side, channels):
        values = jnp.concatenate([held[side, c].astype(jnp.float32) for c in channels])
        square = values * values
        power = jnp.concatenate(
            [with_partner(square[i : i + 8]) for i in range(0, square.shape[0], 8)]
        )
        magnitude = jnp.sqrt(power)
        high = magnitude.astype(jnp.bfloat16)
        rest = magnitude - high.astype(jnp.float32)
        middle = rest.astype(jnp.bfloat16)
        low = (rest - middle.astype(jnp.float32)).astype(jnp.bfloat16)
        smoothed = (
            jnp.dot(
                jnp.concatenate((high, middle, low), axis=1),
                band,
                preferred_element_type=jnp.float32,
            )
            / 5.0
        )
        kept = jnp.concatenate([keep * chan_mask[starts[side] + c].astype(jnp.float32) for c in channels])
        return values * (kept / (smoothed + WATER))

    for side, piece in enumerate((same, other)):
        copies[side].wait()
        for i in range(0, half, BATCH):
            values = whitened(side, range(i, i + BATCH))
            for j in range(0, BATCH, 2):
                pair = interleave(
                    values[j * rows : (j + 1) * rows], values[(j + 1) * rows : (j + 2) * rows]
                )
                piece[i + j] = pair[0].astype(jnp.bfloat16)
                piece[i + j + 1] = pair[1].astype(jnp.bfloat16)


def whiten(spectra, chan_mask, win_mask):
    channels, rows, bins = spectra.shape
    piece = VMEM((channels // 2, rows, bins), jnp.bfloat16)
    return pl.pallas_call(
        whiten_kernel,
        out_shape=(piece, piece),
        in_specs=[
            pl.BlockSpec(memory_space=SMEM),
            pl.BlockSpec(memory_space=SMEM),
            pl.BlockSpec(memory_space=pl.ANY),
        ],
        out_specs=(pl.BlockSpec(memory_space=VMEM),) * 2,
        scratch_shapes=[
            VMEM((2, channels // 2, rows, bins), jnp.bfloat16),
            pltpu.SemaphoreType.DMA((2,)),
        ],
        cost_estimate=SMALL,
        name="whiten",
    )(chan_mask, win_mask, spectra)


def receiver_kernel(same, other, far_same, far_other, weights, flat, wide, held, sems):
    half, rows, bins = same.shape
    copies = [
        pltpu.make_async_copy(piece, held.at[i], sems.at[i])
        for i, piece in enumerate((same, far_other, other, far_same))
    ]
    for copy in copies:
        copy.start()
    mine = lax.axis_index("tm") * half
    theirs = half - mine
    deep = 2 * rows
    for side, start in enumerate((mine, theirs)):
        for h in range(2):
            copies[2 * side + h].wait()
            piece = held.at[2 * side + h]
            for i in range(0, half, 2):
                pair = interleave(piece[i].astype(jnp.float32), piece[i + 1].astype(jnp.float32))
                for j in range(2):
                    at = pl.multiple_of((start + i + j) * deep + h * rows, rows)
                    flat[pl.ds(at, rows), :] = pair[j]
    for w in range(rows):
        real = flat[pl.ds(2 * w, 2 * half, stride=deep), :]
        imag = flat[pl.ds(2 * w + 1, 2 * half, stride=deep), :]
        wide[pl.ds(2 * w, bins, stride=deep), :] = jnp.concatenate((real, imag)).T
        wide[pl.ds(2 * w + 1, bins, stride=deep), :] = jnp.concatenate((imag, -real)).T
    weights[...] = wide[...].astype(jnp.bfloat16)


def receiver_weights(same, other, far_same, far_other):
    half, rows, bins = same.shape
    return pl.pallas_call(
        receiver_kernel,
        out_shape=jax.ShapeDtypeStruct((bins * 2 * rows, 4 * half), jnp.bfloat16),
        in_specs=[pl.BlockSpec(memory_space=pl.ANY)] * 4,
        out_specs=pl.BlockSpec(memory_space=VMEM),
        scratch_shapes=[
            VMEM((2 * half * 2 * rows, bins), jnp.float32),
            VMEM((bins * 2 * rows, 4 * half), jnp.float32),
            VMEM((4, half, rows, bins), jnp.bfloat16),
            pltpu.SemaphoreType.DMA((4,)),
        ],
        compiler_params=pltpu.CompilerParams(vmem_limit_bytes=24 << 20),
        cost_estimate=SMALL,
        name="receiver_weights",
    )(same, other, far_same, far_other)


def stack_kernel(tour, distances, first, steps, table, weights, *refs):
    blocks = len(distances)
    pieces = refs[: 2 * blocks]
    out = refs[2 * blocks + (0 if first else 1)]
    src, turned, cross, done, in_sem, out_sem = refs[2 * blocks + (1 if first else 2) :]
    sources, rows, bins = pieces[0].shape
    count = steps.shape[0]
    ring = len(tour)
    staged = blocks > 1 or first
    lanes = 2 * rows
    per_tile = 128 // lanes
    tiles = GROUP // per_tile
    depth = GROUP * lanes
    pair_rows = 2 * GROUP
    row = lax.broadcasted_iota(jnp.int32, (pair_rows, 128), 0) % GROUP
    col = lax.broadcasted_iota(jnp.int32, (pair_rows, 128), 1) // lanes
    receivers = weights.shape[1] // 2
    me = lax.axis_index("chan")
    folded = tour[1] == 2

    def owner_at(distance):
        at = jnp.where(me % 2 == 0, me // 2, ring - 1 - me // 2) if folded else me
        at = lax.rem(at + distance + ring, ring)
        return jnp.where(at < ring // 2, 2 * at, 2 * (ring - 1 - at) + 1) if folded else at

    owners = [owner_at(d) for d in distances]
    needed = [
        functools.reduce(jnp.logical_or, [steps[k] == owner for k in range(count)])
        for owner in owners
    ]
    part = sources // 2

    def arrival(b, h):
        return pltpu.make_async_copy(pieces[2 * b + h], src.at[b, h], in_sem.at[b, h])

    for b in range(blocks if staged else 0):
        @pl.when(needed[b])
        def _(b=b):
            for h in range(2):
                arrival(b, h).start()

    def departure(b, k, c):
        return pltpu.make_async_copy(
            done.at[b, pl.ds(c * part, part)], out.at[k, pl.ds(c * part, part)], out_sem.at[b, k, c]
        )

    def compute(b, owner):
        for s in range(sources):
            parts = (src[b, 0, s], src[b, 1, s]) if staged else (pieces[0][s], pieces[1][s])
            turned[s // 2, s % 2] = jnp.concatenate(parts * per_tile).T
        for m in range(bins // pair_rows):
            at = m * pair_rows
            sums = []
            for p in range(2):
                mine = turned[:, p, at : at + pair_rows, :]
                wide = jnp.concatenate(
                    [
                        jnp.where(
                            (row == q * per_tile + col)[None], mine, jnp.zeros_like(mine)
                        ).reshape(sources * GROUP, 128)
                        for q in range(tiles)
                    ],
                    axis=1,
                )
                start = (2 * m + p) * depth
                x = jnp.dot(
                    wide, weights[start : start + depth, :], preferred_element_type=jnp.float32
                )
                sums.append(x.reshape(sources, GROUP, 2 * receivers))
            cross[:, at : at + pair_rows, :] = jnp.concatenate(sums, axis=1).astype(jnp.bfloat16)
        for c in range(2):
            turns = [cross[c * part + i].T for i in range(part)]
            left = jnp.concatenate(
                [jnp.concatenate([x[:receivers], x[receivers:]], axis=1) for x in turns]
            )
            y = jnp.dot(left, table[...], preferred_element_type=jnp.float32)
            done[b, c * part : (c + 1) * part] = y.reshape(part, receivers, LAGS).astype(
                jnp.bfloat16
            )
            for k in range(count):
                @pl.when(steps[k] == owner)
                def _(k=k, c=c):
                    departure(b, k, c).start()

    def turn(b, _):
        later = b == blocks - 1
        owner = jnp.where(later, owners[-1], owners[0])

        @pl.when(jnp.where(later, needed[-1], needed[0]))
        def _():
            for i in range(blocks if staged else 0):
                @pl.when(b == i)
                def _(i=i):
                    for h in range(2):
                        arrival(i, h).wait()
            compute(b, owner)
        return 0

    lax.fori_loop(0, blocks, turn, 0)
    for b in range(blocks):
        for k in range(count):
            @pl.when(steps[k] == owners[b])
            def _(b=b, k=k):
                for c in range(2):
                    departure(b, k, c).wait()


def stack(distances, tour, steps, table, weights, pieces, previous, out_shape):
    blocks = len(distances)
    sources, rows, bins = pieces[0].shape
    receivers = weights.shape[1] // 2
    count = steps.shape[0]
    first = previous is None
    if first:
        kinds = [pl.ANY, pl.ANY]
    else:
        kinds = [VMEM if blocks == 1 else pl.ANY] * len(pieces) + [pl.ANY]
    args = [steps, table, weights, *pieces] + ([] if first else [previous])
    return pl.pallas_call(
        functools.partial(stack_kernel, tour, distances, first),
        out_shape=out_shape,
        in_specs=[pl.BlockSpec(memory_space=SMEM)]
        + [pl.BlockSpec(memory_space=VMEM)] * 2
        + [pl.BlockSpec(memory_space=kind) for kind in kinds],
        out_specs=pl.BlockSpec(memory_space=pl.ANY),
        scratch_shapes=[
            VMEM((blocks, 2, sources, rows, bins), jnp.bfloat16),
            VMEM((sources // 2, 2, bins, 128), jnp.bfloat16),
            VMEM((sources, bins, 2 * receivers), jnp.bfloat16),
            VMEM((blocks, sources, receivers, LAGS), jnp.bfloat16),
            pltpu.SemaphoreType.DMA((blocks, 2)),
            pltpu.SemaphoreType.DMA((blocks, count, 2)),
        ],
        input_output_aliases={} if first else {len(args) - 1: 0},
        compiler_params=pltpu.CompilerParams(vmem_limit_bytes=24 << 20),
        cost_estimate=SMALL,
        name="stack",
    )(*args)


def shards(ring, spectra, channel_mask, window_mask, source_block):
    count = len(ring)
    channels, windows, parts, bins = spectra.shape
    steps = source_block.shape[0]
    halves = lax.axis_size("tm")
    rows = spectra.reshape(channels, windows * parts, bins)
    same, other = whiten(rows, channel_mask, window_mask)

    def across(x):
        return lax.ppermute(x, "tm", [(0, 1), (1, 0)])

    def send(x, direction, cross=False):
        pairs = []
        for i in range(count):
            a, b = ring[i], ring[(i + direction) % count]
            for t in range(2):
                pairs.append((2 * a + t, 2 * b + (1 - t if cross else t)))
        return lax.ppermute(x, ("chan", "tm"), pairs)

    table = lag_tables(windows * halves, bins)

    half = count // 2
    tie = lax.optimization_barrier
    early = (send(same, 1), send(same, -1))
    far_same = across(same)
    far_other = across(other)
    late = (send(other, 1, True), send(other, -1, True))
    weights = receiver_weights(same, other, far_same, far_other)
    run = functools.partial(
        stack,
        out_shape=jax.ShapeDtypeStruct((steps, channels // 2, channels, LAGS), jnp.bfloat16),
    )
    rest = (tuple(ring), source_block, table)
    out = None
    held = []
    for hop in range(1, half):
        closing = hop == half - 1
        if hop == 1:
            early, weights = tie((early, weights))
        else:
            early, out = tie((early, out))
        coming = (send(early[0], 1), None if closing else send(early[1], -1))
        if hop == 1:
            late, weights = tie((late, weights))
        held.append((early[0], late[0], early[1], late[1]))
        later = (None if closing else send(late[0], 1), send(late[1], -1))
        if hop == 1:
            out = run((0,), *rest, weights, (same, far_other), None)
        elif not closing:
            late, out = tie((late, out))
            out = run((1 - hop, hop - 1), *rest, weights, held[hop - 2], out)
        early, late = coming, later
    for hop in range(half - 2, half):
        out = run((-hop, hop), *rest, weights, held[hop - 1], out)
    return run((half,), *rest, weights, (early[0], late[1]), out)


def solution(mesh):
    placed = (P(("grp", "chan"), "tm", None, None), P(("grp", "chan")), P(("grp", "tm")), P())
    return jax.shard_map(
        functools.partial(shards, ring_order(mesh)),
        mesh=mesh,
        in_specs=placed,
        out_specs=P(None, "tm", ("grp", "chan"), None),
        check_vma=False,
    )
```

```python
import functools
import math

import jax
import jax.numpy as jnp
import numpy as np
from jax import lax
from jax.experimental import pallas as pl
from jax.experimental.pallas import tpu as pltpu
from jax.sharding import PartitionSpec as P

LAGS = 128
NFFT = 8192
LOW_BIN = 8
LAG_STEP = 28
WATER = 0.1
BATCH = 8
GROUP = 4

VMEM = pltpu.VMEM
SMEM = pltpu.SMEM
SMALL = pl.CostEstimate(flops=1 << 20, bytes_accessed=1 << 14, transcendentals=0)


def ring_order(mesh):
    count = mesh.shape["chan"]
    natural = list(range(count))
    folded = natural[0::2] + natural[1::2][::-1]
    if count % 2:
        return natural
    grid = np.moveaxis(mesh.devices, mesh.axis_names.index("chan"), 0).reshape(count, -1)[:, 0]
    places = [getattr(device, "coords", None) for device in grid]
    if any(place is None for place in places):
        return folded if count == 8 else natural

    def length(tour):
        return sum(
            sum(abs(a - b) for a, b in zip(places[tour[i]], places[tour[i - 1]]))
            for i in range(count)
        )

    return folded if length(folded) < length(natural) else natural


def lag_tables(windows, bins):
    freq = np.arange(bins) + LOW_BIN
    lag = (np.arange(LAGS) - LAGS // 2) * LAG_STEP
    phase = (freq[:, None] * lag[None, :] % NFFT) * (2.0 * math.pi / NFFT)
    table = np.concatenate((np.cos(phase), -np.sin(phase))) / math.sqrt(windows * bins)
    return jnp.asarray(table, jnp.float32).astype(jnp.bfloat16)


def exchange(first, second, size):
    bins = first.shape[-1]
    lane = lax.broadcasted_iota(jnp.int32, first.shape, 1)
    even = lane // size % 2 == 0
    return (
        jnp.where(even, first, pltpu.roll(second, size, 1)),
        jnp.where(even, pltpu.roll(first, bins - size, 1), second),
    )


def interleave(a, b, c, d):
    a, c = exchange(a, c, 2 * GROUP)
    b, d = exchange(b, d, 2 * GROUP)
    return exchange(a, b, GROUP) + exchange(c, d, GROUP)


def whiten_kernel(chan_in, win_in, spectra, same, other, held, chan_mask, win_mask, sems):
    rows, bins = spectra.shape[1:]
    half = same.shape[0]
    own = lax.axis_index("tm") * half
    starts = (own, half - own)
    copies = [
        pltpu.make_async_copy(spectra.at[pl.ds(start, half)], held.at[i], sems.at[i])
        for i, start in enumerate(starts)
    ]
    masks = [
        pltpu.make_async_copy(win_in, win_mask, sems.at[2]),
        pltpu.make_async_copy(chan_in, chan_mask, sems.at[3]),
    ]
    for copy in copies + masks:
        copy.start()
    for copy in masks:
        copy.wait()
    row = lax.broadcasted_iota(jnp.int32, (rows, bins), 0)
    keep = jnp.zeros((rows, bins), jnp.float32)
    for w in range(rows // 2):
        keep = jnp.where(row // 2 == w, win_mask[w].astype(jnp.float32), keep)

    source = lax.broadcasted_iota(jnp.int32, (bins, bins), 0)
    target = lax.broadcasted_iota(jnp.int32, (bins, bins), 1)
    band = sum(
        jnp.where(source == jnp.clip(target + d, 0, bins - 1), 1.0, 0.0) for d in range(-2, 3)
    ).astype(jnp.bfloat16)
    band = jnp.concatenate([band] * 3)

    def with_partner(square):
        even = lax.broadcasted_iota(jnp.int32, square.shape, 0) % 2 == 0
        last = square.shape[0] - 1
        return square + jnp.where(even, pltpu.roll(square, last, 0), pltpu.roll(square, 1, 0))

    def whitened(side, channels):
        values = jnp.concatenate([held[side, c].astype(jnp.float32) for c in channels])
        square = values * values
        power = jnp.concatenate(
            [with_partner(square[i : i + 8]) for i in range(0, square.shape[0], 8)]
        )
        magnitude = jnp.sqrt(power)
        high = magnitude.astype(jnp.bfloat16)
        rest = magnitude - high.astype(jnp.float32)
        middle = rest.astype(jnp.bfloat16)
        low = (rest - middle.astype(jnp.float32)).astype(jnp.bfloat16)
        smoothed = (
            jnp.dot(
                jnp.concatenate((high, middle, low), axis=1),
                band,
                preferred_element_type=jnp.float32,
            )
            / 5.0
        )
        kept = jnp.concatenate([keep * chan_mask[starts[side] + c].astype(jnp.float32) for c in channels])
        return values * (kept / (smoothed + WATER))

    for side, piece in enumerate((same, other)):
        copies[side].wait()
        for i in range(0, half, BATCH):
            values = whitened(side, range(i, i + BATCH))
            for j in range(0, BATCH, GROUP):
                mixed = interleave(
                    *(values[n * rows : (n + 1) * rows] for n in range(j, j + GROUP))
                )
                for n, one in enumerate(mixed):
                    piece[i + j + n] = one.astype(jnp.bfloat16)


def whiten(spectra, chan_mask, win_mask):
    channels, rows, bins = spectra.shape
    piece = VMEM((channels // 2, rows, bins), jnp.bfloat16)
    return pl.pallas_call(
        whiten_kernel,
        out_shape=(piece, piece),
        in_specs=[pl.BlockSpec(memory_space=pl.ANY)] * 3,
        out_specs=(pl.BlockSpec(memory_space=VMEM),) * 2,
        scratch_shapes=[
            VMEM((2, channels // 2, rows, bins), jnp.bfloat16),
            SMEM(chan_mask.shape, chan_mask.dtype),
            SMEM(win_mask.shape, win_mask.dtype),
            pltpu.SemaphoreType.DMA((4,)),
        ],
        cost_estimate=SMALL,
        name="whiten",
    )(chan_mask, win_mask, spectra)


def receiver_kernel(same, other, far_same, far_other, weights, flat, wide, held, sems):
    half, rows, bins = same.shape
    copies = [
        pltpu.make_async_copy(piece, held.at[i], sems.at[i])
        for i, piece in enumerate((same, far_other, other, far_same))
    ]
    for copy in copies:
        copy.start()
    mine = lax.axis_index("tm") * half
    theirs = half - mine
    deep = 2 * rows
    for side, start in enumerate((mine, theirs)):
        for h in range(2):
            copies[2 * side + h].wait()
            piece = held.at[2 * side + h]
            for i in range(0, half, GROUP):
                apart = interleave(*(piece[i + j].astype(jnp.float32) for j in range(GROUP)))
                for j, one in enumerate(apart):
                    at = pl.multiple_of((start + i + j) * deep + h * rows, rows)
                    flat[pl.ds(at, rows), :] = one
    for w in range(rows):
        real = flat[pl.ds(2 * w, 2 * half, stride=deep), :]
        imag = flat[pl.ds(2 * w + 1, 2 * half, stride=deep), :]
        wide[pl.ds(2 * w, bins, stride=deep), :] = jnp.concatenate((real, imag)).T
        wide[pl.ds(2 * w + 1, bins, stride=deep), :] = jnp.concatenate((imag, -real)).T
    weights[...] = wide[...].astype(jnp.bfloat16)


def receiver_weights(same, other, far_same, far_other):
    half, rows, bins = same.shape
    return pl.pallas_call(
        receiver_kernel,
        out_shape=jax.ShapeDtypeStruct((bins * 2 * rows, 4 * half), jnp.bfloat16),
        in_specs=[pl.BlockSpec(memory_space=pl.ANY)] * 4,
        out_specs=pl.BlockSpec(memory_space=VMEM),
        scratch_shapes=[
            VMEM((2 * half * 2 * rows, bins), jnp.float32),
            VMEM((bins * 2 * rows, 4 * half), jnp.float32),
            VMEM((4, half, rows, bins), jnp.bfloat16),
            pltpu.SemaphoreType.DMA((4,)),
        ],
        compiler_params=pltpu.CompilerParams(vmem_limit_bytes=24 << 20),
        cost_estimate=SMALL,
        name="receiver_weights",
    )(same, other, far_same, far_other)


def stack_kernel(tour, distances, first, steps_in, table, weights, *refs):
    blocks = len(distances)
    pieces = refs[: 2 * blocks]
    out = refs[2 * blocks + (0 if first else 1)]
    steps, src, turned, cross, done, in_sem, out_sem, step_sem = refs[
        2 * blocks + (1 if first else 2) :
    ]
    sources, rows, bins = pieces[0].shape
    count = steps.shape[0]
    ring = len(tour)
    staged = blocks > 1 or first
    lanes = 2 * rows
    per_tile = 128 // lanes
    tiles = GROUP // per_tile
    depth = GROUP * lanes
    span = GROUP * GROUP
    row = lax.broadcasted_iota(jnp.int32, (span, 128), 0) % GROUP
    col = lax.broadcasted_iota(jnp.int32, (span, 128), 1) // lanes
    receivers = weights.shape[1] // 2
    me = lax.axis_index("chan")
    folded = tour[1] == 2

    def owner_at(distance):
        at = jnp.where(me % 2 == 0, me // 2, ring - 1 - me // 2) if folded else me
        at = lax.rem(at + distance + ring, ring)
        return jnp.where(at < ring // 2, 2 * at, 2 * (ring - 1 - at) + 1) if folded else at

    owners = [owner_at(d) for d in distances]
    parts_out = out_sem.shape[2]
    part = sources // parts_out
    asked = pltpu.make_async_copy(steps_in, steps, step_sem)
    asked.start()
    if staged:
        asked.wait()
        needed = [
            functools.reduce(jnp.logical_or, [steps[k] == owner for k in range(count)])
            for owner in owners
        ]

    def arrival(b, h):
        return pltpu.make_async_copy(pieces[2 * b + h], src.at[b, h], in_sem.at[b, h])

    for b in range(blocks if staged else 0):
        @pl.when(needed[b])
        def _(b=b):
            for h in range(2):
                arrival(b, h).start()

    def departure(b, k, c):
        return pltpu.make_async_copy(
            done.at[b, pl.ds(c * part, part)], out.at[k, pl.ds(c * part, part)], out_sem.at[b, k, c]
        )

    def compute(b, owner):
        for s in range(sources):
            parts = (src[b, 0, s], src[b, 1, s]) if staged else (pieces[0][s], pieces[1][s])
            turned[s // GROUP, s % GROUP] = jnp.concatenate(parts * per_tile).T
        for m in range(bins // span):
            at = m * span
            sums = []
            for p in range(GROUP):
                mine = turned[:, p, at : at + span, :]
                wide = jnp.concatenate(
                    [
                        jnp.where(
                            (row == q * per_tile + col)[None], mine, jnp.zeros_like(mine)
                        ).reshape(sources * GROUP, 128)
                        for q in range(tiles)
                    ],
                    axis=1,
                )
                start = (GROUP * m + p) * depth
                x = jnp.dot(
                    wide, weights[start : start + depth, :], preferred_element_type=jnp.float32
                )
                sums.append(x.reshape(sources // 2, 2 * GROUP, 2 * receivers))
            eights = []
            for p in range(0, GROUP, 2):
                low, high = sums[p], sums[p + 1]
                upper = lax.broadcasted_iota(jnp.int32, low.shape, 1) < GROUP
                one = jnp.where(upper, low, pltpu.roll(high, GROUP, 1))
                two = jnp.where(upper, pltpu.roll(low, GROUP, 1), high)
                eights.append(
                    jnp.stack((one, two), axis=1).reshape(sources, 2 * GROUP, 2 * receivers)
                )
            cross[:, at : at + span, :] = jnp.concatenate(eights, axis=1).astype(jnp.bfloat16)
        if not staged:
            asked.wait()
        for c in range(parts_out):
            turns = [cross[c * part + i].T for i in range(part)]
            left = jnp.concatenate(
                [jnp.concatenate([x[:receivers], x[receivers:]], axis=1) for x in turns]
            )
            y = jnp.dot(left, table[...], preferred_element_type=jnp.float32)
            done[b, c * part : (c + 1) * part] = y.reshape(part, receivers, LAGS).astype(
                jnp.bfloat16
            )
            for k in range(count):
                @pl.when(steps[k] == owner)
                def _(k=k, c=c):
                    departure(b, k, c).start()

    def turn(b, _):
        later = b == blocks - 1
        owner = jnp.where(later, owners[-1], owners[0])

        @pl.when(jnp.where(later, needed[-1], needed[0]))
        def _():
            for i in range(blocks if staged else 0):
                @pl.when(b == i)
                def _(i=i):
                    for h in range(2):
                        arrival(i, h).wait()
            compute(b, owner)
        return 0

    if staged:
        lax.fori_loop(0, blocks, turn, 0)
    else:
        compute(0, owners[0])
    for b in range(blocks):
        for k in range(count):
            @pl.when(steps[k] == owners[b])
            def _(b=b, k=k):
                for c in range(parts_out):
                    departure(b, k, c).wait()


def stack(distances, tour, steps, table, weights, pieces, previous, out_shape):
    blocks = len(distances)
    sources, rows, bins = pieces[0].shape
    receivers = weights.shape[1] // 2
    count = steps.shape[0]
    first = previous is None
    if first:
        kinds = [pl.ANY, pl.ANY]
    else:
        kinds = [VMEM if blocks == 1 else pl.ANY] * len(pieces) + [pl.ANY]
    args = [steps, table, weights, *pieces] + ([] if first else [previous])
    return pl.pallas_call(
        functools.partial(stack_kernel, tour, distances, first),
        out_shape=out_shape,
        in_specs=[pl.BlockSpec(memory_space=pl.ANY)]
        + [pl.BlockSpec(memory_space=VMEM)] * 2
        + [pl.BlockSpec(memory_space=kind) for kind in kinds],
        out_specs=pl.BlockSpec(memory_space=pl.ANY),
        scratch_shapes=[
            SMEM(steps.shape, steps.dtype),
            VMEM((blocks, 2, sources, rows, bins), jnp.bfloat16),
            VMEM((sources // GROUP, GROUP, bins, 128), jnp.bfloat16),
            VMEM((sources, bins, 2 * receivers), jnp.bfloat16),
            VMEM((blocks, sources, receivers, LAGS), jnp.bfloat16),
            pltpu.SemaphoreType.DMA((blocks, 2)),
            pltpu.SemaphoreType.DMA((blocks, count, 4 if blocks == 1 else 2)),
            pltpu.SemaphoreType.DMA,
        ],
        input_output_aliases={} if first else {len(args) - 1: 0},
        compiler_params=pltpu.CompilerParams(vmem_limit_bytes=24 << 20),
        cost_estimate=SMALL,
        name="stack",
    )(*args)


def shards(ring, spectra, channel_mask, window_mask, source_block):
    count = len(ring)
    channels, windows, parts, bins = spectra.shape
    steps = source_block.shape[0]
    halves = lax.axis_size("tm")
    rows = spectra.reshape(channels, windows * parts, bins)
    same, other = whiten(rows, channel_mask, window_mask)

    def across(x):
        return lax.ppermute(x, "tm", [(0, 1), (1, 0)])

    def send(x, direction, cross=False):
        pairs = []
        for i in range(count):
            a, b = ring[i], ring[(i + direction) % count]
            for t in range(2):
                pairs.append((2 * a + t, 2 * b + (1 - t if cross else t)))
        return lax.ppermute(x, ("chan", "tm"), pairs)

    table = lag_tables(windows * halves, bins)

    half = count // 2
    tie = lax.optimization_barrier
    early = (send(same, 1), send(same, -1))
    far_same = across(same)
    far_other = across(other)
    late = (send(other, 1, True), send(other, -1, True))
    weights = receiver_weights(same, other, far_same, far_other)
    run = functools.partial(
        stack,
        out_shape=jax.ShapeDtypeStruct((steps, channels // 2, channels, LAGS), jnp.bfloat16),
    )
    rest = (tuple(ring), source_block, table)
    out = None
    held = []
    for hop in range(1, half):
        closing = hop == half - 1
        if hop == 1:
            early, weights = tie((early, weights))
        else:
            early, out = tie((early, out))
        coming = (send(early[0], 1), None if closing else send(early[1], -1))
        if hop == 1:
            late, weights = tie((late, weights))
        held.append((early[0], late[0], early[1], late[1]))
        later = (None if closing else send(late[0], 1), send(late[1], -1))
        if hop == 1:
            out = run((0,), *rest, weights, (same, far_other), None)
        elif not closing:
            late, out = tie((late, out))
            out = run((1 - hop, hop - 1), *rest, weights, held[hop - 2], out)
        early, late = coming, later
    for hop in range(half - 2, half):
        out = run((-hop, hop), *rest, weights, held[hop - 1], out)
    return run((half,), *rest, weights, (early[0], late[1]), out)


def solution(mesh):
    placed = (P(("grp", "chan"), "tm", None, None), P(("grp", "chan")), P(("grp", "tm")), P())
    return jax.shard_map(
        functools.partial(shards, ring_order(mesh)),
        mesh=mesh,
        in_specs=placed,
        out_specs=P(None, "tm", ("grp", "chan"), None),
        check_vma=False,
    )
```

```python
import functools
import math

import jax
import jax.numpy as jnp
import numpy as np
from jax import lax
from jax.experimental import pallas as pl
from jax.experimental.pallas import tpu as pltpu
from jax.sharding import PartitionSpec as P

LAGS = 128
NFFT = 8192
LOW_BIN = 8
LAG_STEP = 28
WATER = 0.1
BATCH = 8
GROUP = 4

VMEM = pltpu.VMEM
SMEM = pltpu.SMEM
SMALL = pl.CostEstimate(flops=1 << 20, bytes_accessed=1 << 14, transcendentals=0)


def ring_order(mesh):
    count = mesh.shape["chan"]
    natural = list(range(count))
    folded = natural[0::2] + natural[1::2][::-1]
    if count % 2:
        return natural
    grid = np.moveaxis(mesh.devices, mesh.axis_names.index("chan"), 0).reshape(count, -1)[:, 0]
    places = [getattr(device, "coords", None) for device in grid]
    if any(place is None for place in places):
        return folded if count == 8 else natural

    def length(tour):
        return sum(
            sum(abs(a - b) for a, b in zip(places[tour[i]], places[tour[i - 1]]))
            for i in range(count)
        )

    return folded if length(folded) < length(natural) else natural


def lag_tables(windows, bins):
    freq = np.arange(bins) + LOW_BIN
    lag = (np.arange(LAGS) - LAGS // 2) * LAG_STEP
    phase = (freq[:, None] * lag[None, :] % NFFT) * (2.0 * math.pi / NFFT)
    table = np.concatenate((np.cos(phase), -np.sin(phase))) / math.sqrt(windows * bins)
    return jnp.asarray(table, jnp.float32).astype(jnp.bfloat16)


def exchange(first, second, size):
    bins = first.shape[-1]
    lane = lax.broadcasted_iota(jnp.int32, first.shape, 1)
    even = lane // size % 2 == 0
    return (
        jnp.where(even, first, pltpu.roll(second, size, 1)),
        jnp.where(even, pltpu.roll(first, bins - size, 1), second),
    )


def interleave(a, b, c, d):
    a, c = exchange(a, c, 2 * GROUP)
    b, d = exchange(b, d, 2 * GROUP)
    return exchange(a, b, GROUP) + exchange(c, d, GROUP)


def whiten_kernel(chan_in, win_in, spectra, same, other, held, chan_mask, win_mask, sems):
    rows, bins = spectra.shape[1:]
    half = same.shape[0]
    own = lax.axis_index("tm") * half
    starts = (own, half - own)
    copies = [
        pltpu.make_async_copy(spectra.at[pl.ds(start, half)], held.at[i], sems.at[i])
        for i, start in enumerate(starts)
    ]
    masks = [
        pltpu.make_async_copy(win_in, win_mask, sems.at[2]),
        pltpu.make_async_copy(chan_in, chan_mask, sems.at[3]),
    ]
    for copy in copies + masks:
        copy.start()
    for copy in masks:
        copy.wait()
    row = lax.broadcasted_iota(jnp.int32, (rows, bins), 0)
    keep = jnp.zeros((rows, bins), jnp.float32)
    for w in range(rows // 2):
        keep = jnp.where(row // 2 == w, win_mask[w].astype(jnp.float32), keep)

    source = lax.broadcasted_iota(jnp.int32, (bins, bins), 0)
    target = lax.broadcasted_iota(jnp.int32, (bins, bins), 1)
    band = sum(
        jnp.where(source == jnp.clip(target + d, 0, bins - 1), 1.0, 0.0) for d in range(-2, 3)
    ).astype(jnp.bfloat16)
    band = jnp.concatenate([band] * 3)

    def with_partner(square):
        even = lax.broadcasted_iota(jnp.int32, square.shape, 0) % 2 == 0
        last = square.shape[0] - 1
        return square + jnp.where(even, pltpu.roll(square, last, 0), pltpu.roll(square, 1, 0))

    def whitened(side, channels):
        values = jnp.concatenate([held[side, c].astype(jnp.float32) for c in channels])
        square = values * values
        power = jnp.concatenate(
            [with_partner(square[i : i + 8]) for i in range(0, square.shape[0], 8)]
        )
        magnitude = jnp.sqrt(power)
        high = magnitude.astype(jnp.bfloat16)
        rest = magnitude - high.astype(jnp.float32)
        middle = rest.astype(jnp.bfloat16)
        low = (rest - middle.astype(jnp.float32)).astype(jnp.bfloat16)
        smoothed = (
            jnp.dot(
                jnp.concatenate((high, middle, low), axis=1),
                band,
                preferred_element_type=jnp.float32,
            )
            / 5.0
        )
        kept = jnp.concatenate([keep * chan_mask[starts[side] + c].astype(jnp.float32) for c in channels])
        return values * (kept / (smoothed + WATER))

    for side, piece in enumerate((same, other)):
        copies[side].wait()
        for i in range(0, half, BATCH):
            values = whitened(side, range(i, i + BATCH))
            for j in range(0, BATCH, GROUP):
                mixed = interleave(
                    *(values[n * rows : (n + 1) * rows] for n in range(j, j + GROUP))
                )
                for n, one in enumerate(mixed):
                    piece[i + j + n] = one.astype(jnp.bfloat16)


def whiten(spectra, chan_mask, win_mask):
    channels, rows, bins = spectra.shape
    piece = VMEM((channels // 2, rows, bins), jnp.bfloat16)
    return pl.pallas_call(
        whiten_kernel,
        out_shape=(piece, piece),
        in_specs=[pl.BlockSpec(memory_space=pl.ANY)] * 3,
        out_specs=(pl.BlockSpec(memory_space=VMEM),) * 2,
        scratch_shapes=[
            VMEM((2, channels // 2, rows, bins), jnp.bfloat16),
            SMEM(chan_mask.shape, chan_mask.dtype),
            SMEM(win_mask.shape, win_mask.dtype),
            pltpu.SemaphoreType.DMA((4,)),
        ],
        cost_estimate=SMALL,
        name="whiten",
    )(chan_mask, win_mask, spectra)


def receiver_kernel(same, other, far_same, far_other, weights, flat, wide, held, sems):
    half, rows, bins = same.shape
    copies = [
        pltpu.make_async_copy(piece, held.at[i], sems.at[i])
        for i, piece in enumerate((same, far_other, other, far_same))
    ]
    for copy in copies:
        copy.start()
    mine = lax.axis_index("tm") * half
    theirs = half - mine
    deep = 2 * rows
    for side, start in enumerate((mine, theirs)):
        for h in range(2):
            copies[2 * side + h].wait()
            piece = held.at[2 * side + h]
            for i in range(0, half, GROUP):
                apart = interleave(*(piece[i + j].astype(jnp.float32) for j in range(GROUP)))
                for j, one in enumerate(apart):
                    at = pl.multiple_of((start + i + j) * deep + h * rows, rows)
                    flat[pl.ds(at, rows), :] = one
    for w in range(rows):
        real = flat[pl.ds(2 * w, 2 * half, stride=deep), :]
        imag = flat[pl.ds(2 * w + 1, 2 * half, stride=deep), :]
        wide[pl.ds(2 * w, bins, stride=deep), :] = jnp.concatenate((real, imag)).T
        wide[pl.ds(2 * w + 1, bins, stride=deep), :] = jnp.concatenate((imag, -real)).T
    weights[...] = wide[...].astype(jnp.bfloat16)


def receiver_weights(same, other, far_same, far_other):
    half, rows, bins = same.shape
    return pl.pallas_call(
        receiver_kernel,
        out_shape=jax.ShapeDtypeStruct((bins * 2 * rows, 4 * half), jnp.bfloat16),
        in_specs=[pl.BlockSpec(memory_space=pl.ANY)] * 4,
        out_specs=pl.BlockSpec(memory_space=VMEM),
        scratch_shapes=[
            VMEM((2 * half * 2 * rows, bins), jnp.float32),
            VMEM((bins * 2 * rows, 4 * half), jnp.float32),
            VMEM((4, half, rows, bins), jnp.bfloat16),
            pltpu.SemaphoreType.DMA((4,)),
        ],
        compiler_params=pltpu.CompilerParams(vmem_limit_bytes=24 << 20),
        cost_estimate=SMALL,
        name="receiver_weights",
    )(same, other, far_same, far_other)


def stack_kernel(tour, distances, first, steps_in, table, weights, *refs):
    blocks = len(distances)
    pieces = refs[: 2 * blocks]
    out = refs[2 * blocks + (0 if first else 1)]
    steps, src, turned, cross, done, in_sem, out_sem, step_sem = refs[
        2 * blocks + (1 if first else 2) :
    ]
    sources, rows, bins = pieces[0].shape
    count = steps.shape[0]
    ring = len(tour)
    staged = blocks > 1 or first
    lanes = 2 * rows
    per_tile = 128 // lanes
    tiles = GROUP // per_tile
    depth = GROUP * lanes
    span = GROUP * GROUP
    row = lax.broadcasted_iota(jnp.int32, (span, 128), 0) % GROUP
    col = lax.broadcasted_iota(jnp.int32, (span, 128), 1) // lanes
    receivers = weights.shape[1] // 2
    me = lax.axis_index("chan")
    folded = tour[1] == 2

    def owner_at(distance):
        at = jnp.where(me % 2 == 0, me // 2, ring - 1 - me // 2) if folded else me
        at = lax.rem(at + distance + ring, ring)
        return jnp.where(at < ring // 2, 2 * at, 2 * (ring - 1 - at) + 1) if folded else at

    owners = [owner_at(d) for d in distances]
    parts_out = out_sem.shape[2]
    part = sources // parts_out
    asked = pltpu.make_async_copy(steps_in, steps, step_sem)
    asked.start()
    if staged:
        asked.wait()
        needed = [
            functools.reduce(jnp.logical_or, [steps[k] == owner for k in range(count)])
            for owner in owners
        ]

    def arrival(b, h):
        return pltpu.make_async_copy(pieces[2 * b + h], src.at[b, h], in_sem.at[b, h])

    for b in range(blocks if staged else 0):
        @pl.when(needed[b])
        def _(b=b):
            for h in range(2):
                arrival(b, h).start()

    def departure(b, k, c):
        return pltpu.make_async_copy(
            done.at[b, pl.ds(c * part, part)], out.at[k, pl.ds(c * part, part)], out_sem.at[b, k, c]
        )

    def compute(b, owner):
        for s in range(sources):
            parts = (src[b, 0, s], src[b, 1, s]) if staged else (pieces[0][s], pieces[1][s])
            turned[s // GROUP, s % GROUP] = jnp.concatenate(parts * per_tile).T
        for m in range(bins // span):
            at = m * span
            sums = []
            for p in range(GROUP):
                mine = turned[:, p, at : at + span, :]
                wide = jnp.concatenate(
                    [
                        jnp.where(
                            (row == q * per_tile + col)[None], mine, jnp.zeros_like(mine)
                        ).reshape(sources * GROUP, 128)
                        for q in range(tiles)
                    ],
                    axis=1,
                )
                start = (GROUP * m + p) * depth
                x = jnp.dot(
                    wide, weights[start : start + depth, :], preferred_element_type=jnp.float32
                )
                sums.append(x.reshape(sources // 2, 2 * GROUP, 2 * receivers))
            eights = []
            for p in range(0, GROUP, 2):
                low, high = sums[p], sums[p + 1]
                upper = lax.broadcasted_iota(jnp.int32, low.shape, 1) < GROUP
                one = jnp.where(upper, low, pltpu.roll(high, GROUP, 1))
                two = jnp.where(upper, pltpu.roll(low, GROUP, 1), high)
                eights.append(
                    jnp.stack((one, two), axis=1).reshape(sources, 2 * GROUP, 2 * receivers)
                )
            cross[:, at : at + span, :] = jnp.concatenate(eights, axis=1).astype(jnp.bfloat16)
        if not staged:
            asked.wait()
        for c in range(parts_out):
            turns = [cross[c * part + i].T for i in range(part)]
            left = jnp.concatenate(
                [jnp.concatenate([x[:receivers], x[receivers:]], axis=1) for x in turns]
            )
            y = jnp.dot(left, table[...], preferred_element_type=jnp.float32)
            done[b, c * part : (c + 1) * part] = y.reshape(part, receivers, LAGS).astype(
                jnp.bfloat16
            )
            for k in range(count):
                @pl.when(steps[k] == owner)
                def _(k=k, c=c):
                    departure(b, k, c).start()

    def turn(b, _):
        later = b == blocks - 1
        owner = jnp.where(later, owners[-1], owners[0])

        @pl.when(jnp.where(later, needed[-1], needed[0]))
        def _():
            for i in range(blocks if staged else 0):
                @pl.when(b == i)
                def _(i=i):
                    for h in range(2):
                        arrival(i, h).wait()
            compute(b, owner)
        return 0

    if staged:
        lax.fori_loop(0, blocks, turn, 0)
    else:
        compute(0, owners[0])
    for b in range(blocks):
        for k in range(count):
            @pl.when(steps[k] == owners[b])
            def _(b=b, k=k):
                for c in range(parts_out):
                    departure(b, k, c).wait()


def stack(distances, tour, steps, table, weights, pieces, previous, out_shape):
    blocks = len(distances)
    sources, rows, bins = pieces[0].shape
    receivers = weights.shape[1] // 2
    count = steps.shape[0]
    first = previous is None
    if first:
        kinds = [pl.ANY, pl.ANY]
    else:
        kinds = [VMEM if blocks == 1 else pl.ANY] * len(pieces) + [pl.ANY]
    args = [steps, table, weights, *pieces] + ([] if first else [previous])
    return pl.pallas_call(
        functools.partial(stack_kernel, tour, distances, first),
        out_shape=out_shape,
        in_specs=[pl.BlockSpec(memory_space=pl.ANY)]
        + [pl.BlockSpec(memory_space=VMEM)] * 2
        + [pl.BlockSpec(memory_space=kind) for kind in kinds],
        out_specs=pl.BlockSpec(memory_space=pl.ANY),
        scratch_shapes=[
            SMEM(steps.shape, steps.dtype),
            VMEM((blocks, 2, sources, rows, bins), jnp.bfloat16),
            VMEM((sources // GROUP, GROUP, bins, 128), jnp.bfloat16),
            VMEM((sources, bins, 2 * receivers), jnp.bfloat16),
            VMEM((blocks, sources, receivers, LAGS), jnp.bfloat16),
            pltpu.SemaphoreType.DMA((blocks, 2)),
            pltpu.SemaphoreType.DMA((blocks, count, 4 if blocks == 1 else 2)),
            pltpu.SemaphoreType.DMA,
        ],
        input_output_aliases={} if first else {len(args) - 1: 0},
        compiler_params=pltpu.CompilerParams(vmem_limit_bytes=24 << 20),
        cost_estimate=SMALL,
        name="stack",
    )(*args)


def shards(ring, spectra, channel_mask, window_mask, source_block):
    count = len(ring)
    channels, windows, parts, bins = spectra.shape
    steps = source_block.shape[0]
    halves = lax.axis_size("tm")
    rows = spectra.reshape(channels, windows * parts, bins)
    same, other = whiten(rows, channel_mask, window_mask)

    def across(x):
        return lax.ppermute(x, "tm", [(0, 1), (1, 0)])

    def send(x, direction, cross=False):
        pairs = []
        for i in range(count):
            a, b = ring[i], ring[(i + direction) % count]
            for t in range(2):
                pairs.append((2 * a + t, 2 * b + (1 - t if cross else t)))
        return lax.ppermute(x, ("chan", "tm"), pairs)

    table = lag_tables(windows * halves, bins)

    half = count // 2
    early = [send(same, 1), send(other, -1, True)]
    far_same = across(same)
    far_other = across(other)
    late = [send(other, 1, True), send(same, -1)]
    weights = receiver_weights(same, other, far_same, far_other)
    run = functools.partial(
        stack,
        out_shape=jax.ShapeDtypeStruct((steps, channels // 2, channels, LAGS), jnp.bfloat16),
    )
    rest = (tuple(ring), source_block, table)

    def tie(pieces, token):
        tied = []
        for piece in pieces:
            piece, token = lax.optimization_barrier((piece, token))
            tied.append(piece)
        return tied, token

    out = None
    held = []
    for hop in range(1, half):
        closing = hop == half - 1
        if hop == 1:
            early, weights = tie(early, weights)
        else:
            early, out = tie(early, out)
        coming = [send(early[0], 1), send(early[1], -1)]
        if hop == 1:
            late, weights = tie(late, weights)
        held.append((early[0], late[0], late[1], early[1]))
        if not closing:
            later = [send(late[0], 1), send(late[1], -1)]
        if hop == 1:
            out = run((0,), *rest, weights, (same, far_other), None)
        elif not closing:
            late, out = tie(late, out)
            out = run((1 - hop, hop - 1), *rest, weights, held[hop - 2], out)
        early, late = coming, later
    for hop in range(half - 2, half):
        out = run((-hop, hop), *rest, weights, held[hop - 1], out)
    return run((half,), *rest, weights, early, out)


def solution(mesh):
    placed = (P(("grp", "chan"), "tm", None, None), P(("grp", "chan")), P(("grp", "tm")), P())
    return jax.shard_map(
        functools.partial(shards, ring_order(mesh)),
        mesh=mesh,
        in_specs=placed,
        out_specs=P(None, "tm", ("grp", "chan"), None),
        check_vma=False,
    )
```

```python
import functools
import math

import jax
import jax.numpy as jnp
import numpy as np
from jax import lax
from jax.experimental import pallas as pl
from jax.experimental.pallas import tpu as pltpu
from jax.sharding import PartitionSpec as P

LAGS = 128
NFFT = 8192
LOW_BIN = 8
LAG_STEP = 28
WATER = 0.1
BATCH = 8
GROUP = 4

VMEM = pltpu.VMEM
SMEM = pltpu.SMEM
SMALL = pl.CostEstimate(flops=1 << 20, bytes_accessed=1 << 14, transcendentals=0)


def ring_order(mesh):
    count = mesh.shape["chan"]
    natural = list(range(count))
    folded = natural[0::2] + natural[1::2][::-1]
    if count % 2:
        return natural
    grid = np.moveaxis(mesh.devices, mesh.axis_names.index("chan"), 0).reshape(count, -1)[:, 0]
    places = [getattr(device, "coords", None) for device in grid]
    if any(place is None for place in places):
        return folded if count == 8 else natural

    def length(tour):
        return sum(
            sum(abs(a - b) for a, b in zip(places[tour[i]], places[tour[i - 1]]))
            for i in range(count)
        )

    return folded if length(folded) < length(natural) else natural


def lag_tables(windows, bins):
    freq = np.arange(bins) + LOW_BIN
    lag = (np.arange(LAGS) - LAGS // 2) * LAG_STEP
    phase = (freq[:, None] * lag[None, :] % NFFT) * (2.0 * math.pi / NFFT)
    table = np.concatenate((np.cos(phase), -np.sin(phase))) / math.sqrt(windows * bins)
    return jnp.asarray(table, jnp.float32).astype(jnp.bfloat16)


def exchange(first, second, size):
    bins = first.shape[-1]
    lane = lax.broadcasted_iota(jnp.int32, first.shape, 1)
    even = lane // size % 2 == 0
    return (
        jnp.where(even, first, pltpu.roll(second, size, 1)),
        jnp.where(even, pltpu.roll(first, bins - size, 1), second),
    )


def interleave(a, b, c, d):
    a, c = exchange(a, c, 2 * GROUP)
    b, d = exchange(b, d, 2 * GROUP)
    return exchange(a, b, GROUP) + exchange(c, d, GROUP)


def whiten_kernel(chan_in, win_in, spectra, same, other, both, held, chan_mask, win_mask, sems):
    rows, bins = spectra.shape[1:]
    half = same.shape[0]
    own = lax.axis_index("tm") * half
    starts = (own, half - own)
    copies = [
        pltpu.make_async_copy(spectra.at[pl.ds(start, half)], held.at[i], sems.at[i])
        for i, start in enumerate(starts)
    ]
    masks = [
        pltpu.make_async_copy(win_in, win_mask, sems.at[2]),
        pltpu.make_async_copy(chan_in, chan_mask, sems.at[3]),
    ]
    for copy in copies + masks:
        copy.start()
    for copy in masks:
        copy.wait()
    row = lax.broadcasted_iota(jnp.int32, (rows, bins), 0)
    keep = jnp.zeros((rows, bins), jnp.float32)
    for w in range(rows // 2):
        keep = jnp.where(row // 2 == w, win_mask[w].astype(jnp.float32), keep)

    source = lax.broadcasted_iota(jnp.int32, (bins, bins), 0)
    target = lax.broadcasted_iota(jnp.int32, (bins, bins), 1)
    band = sum(
        jnp.where(source == jnp.clip(target + d, 0, bins - 1), 1.0, 0.0) for d in range(-2, 3)
    ).astype(jnp.bfloat16)
    band = jnp.concatenate([band] * 3)

    def with_partner(square):
        even = lax.broadcasted_iota(jnp.int32, square.shape, 0) % 2 == 0
        last = square.shape[0] - 1
        return square + jnp.where(even, pltpu.roll(square, last, 0), pltpu.roll(square, 1, 0))

    def whitened(side, channels):
        values = jnp.concatenate([held[side, c].astype(jnp.float32) for c in channels])
        square = values * values
        power = jnp.concatenate(
            [with_partner(square[i : i + 8]) for i in range(0, square.shape[0], 8)]
        )
        magnitude = jnp.sqrt(power)
        high = magnitude.astype(jnp.bfloat16)
        rest = magnitude - high.astype(jnp.float32)
        middle = rest.astype(jnp.bfloat16)
        low = (rest - middle.astype(jnp.float32)).astype(jnp.bfloat16)
        smoothed = (
            jnp.dot(
                jnp.concatenate((high, middle, low), axis=1),
                band,
                preferred_element_type=jnp.float32,
            )
            / 5.0
        )
        kept = jnp.concatenate([keep * chan_mask[starts[side] + c].astype(jnp.float32) for c in channels])
        return values * (kept / (smoothed + WATER))

    for side, piece in enumerate((same, other)):
        copies[side].wait()
        for i in range(0, half, BATCH):
            values = whitened(side, range(i, i + BATCH))
            for j in range(0, BATCH, GROUP):
                mixed = interleave(
                    *(values[n * rows : (n + 1) * rows] for n in range(j, j + GROUP))
                )
                for n, one in enumerate(mixed):
                    one = one.astype(jnp.bfloat16)
                    piece[i + j + n] = one
                    both[side * half + i + j + n] = one


def whiten(spectra, chan_mask, win_mask):
    channels, rows, bins = spectra.shape
    piece = VMEM((channels // 2, rows, bins), jnp.bfloat16)
    return pl.pallas_call(
        whiten_kernel,
        out_shape=(piece, piece, VMEM((channels, rows, bins), jnp.bfloat16)),
        in_specs=[pl.BlockSpec(memory_space=pl.ANY)] * 3,
        out_specs=(pl.BlockSpec(memory_space=VMEM),) * 3,
        scratch_shapes=[
            VMEM((2, channels // 2, rows, bins), jnp.bfloat16),
            SMEM(chan_mask.shape, chan_mask.dtype),
            SMEM(win_mask.shape, win_mask.dtype),
            pltpu.SemaphoreType.DMA((4,)),
        ],
        cost_estimate=SMALL,
        name="whiten",
    )(chan_mask, win_mask, spectra)


def receiver_kernel(both, far, weights, flat, wide, held, sems):
    half, rows, bins = held.shape[1:]
    copies = [
        pltpu.make_async_copy(piece.at[pl.ds(start, half)], held.at[i], sems.at[i])
        for i, (piece, start) in enumerate(((both, 0), (far, half), (both, half), (far, 0)))
    ]
    for copy in copies:
        copy.start()
    mine = lax.axis_index("tm") * half
    theirs = half - mine
    deep = 2 * rows
    for side, start in enumerate((mine, theirs)):
        for h in range(2):
            copies[2 * side + h].wait()
            piece = held.at[2 * side + h]
            for i in range(0, half, GROUP):
                apart = interleave(*(piece[i + j].astype(jnp.float32) for j in range(GROUP)))
                for j, one in enumerate(apart):
                    at = pl.multiple_of((start + i + j) * deep + h * rows, rows)
                    flat[pl.ds(at, rows), :] = one
    for w in range(rows):
        real = flat[pl.ds(2 * w, 2 * half, stride=deep), :]
        imag = flat[pl.ds(2 * w + 1, 2 * half, stride=deep), :]
        wide[pl.ds(2 * w, bins, stride=deep), :] = jnp.concatenate((real, imag)).T
        wide[pl.ds(2 * w + 1, bins, stride=deep), :] = jnp.concatenate((imag, -real)).T
    weights[...] = wide[...].astype(jnp.bfloat16)


def receiver_weights(both, far):
    channels, rows, bins = both.shape
    half = channels // 2
    return pl.pallas_call(
        receiver_kernel,
        out_shape=jax.ShapeDtypeStruct((bins * 2 * rows, 4 * half), jnp.bfloat16),
        in_specs=[pl.BlockSpec(memory_space=pl.ANY)] * 2,
        out_specs=pl.BlockSpec(memory_space=VMEM),
        scratch_shapes=[
            VMEM((2 * half * 2 * rows, bins), jnp.float32),
            VMEM((bins * 2 * rows, 4 * half), jnp.float32),
            VMEM((4, half, rows, bins), jnp.bfloat16),
            pltpu.SemaphoreType.DMA((4,)),
        ],
        compiler_params=pltpu.CompilerParams(vmem_limit_bytes=24 << 20),
        cost_estimate=SMALL,
        name="receiver_weights",
    )(both, far)


def stack_kernel(tour, distances, first, offset, steps_in, table, weights, *refs):
    blocks = len(distances)
    pieces = refs[: 2 * blocks]
    out = refs[2 * blocks + (0 if first else 1)]
    steps, turned, cross, done, out_sem, step_sem = refs[2 * blocks + (1 if first else 2) :]
    sources, receivers, _ = done.shape[1:]
    rows, bins = pieces[0].shape[1:]
    count = steps.shape[0]
    ring = len(tour)
    alone = blocks == 1 and not first
    lanes = 2 * rows
    per_tile = 128 // lanes
    tiles = GROUP // per_tile
    depth = GROUP * lanes
    span = GROUP * GROUP
    row = lax.broadcasted_iota(jnp.int32, (span, 128), 0) % GROUP
    col = lax.broadcasted_iota(jnp.int32, (span, 128), 1) // lanes
    near = pieces[0::2]
    far = [piece.at[pl.ds(sources, sources)] if first else piece for piece in pieces[1::2]]
    me = lax.axis_index("chan")
    folded = tour[1] == 2

    def owner_at(distance):
        at = jnp.where(me % 2 == 0, me // 2, ring - 1 - me // 2) if folded else me
        at = lax.rem(at + distance + ring, ring)
        return jnp.where(at < ring // 2, 2 * at, 2 * (ring - 1 - at) + 1) if folded else at

    owners = [owner_at(d) for d in distances]
    parts_out = out_sem.shape[2]
    part = sources // parts_out
    asked = pltpu.make_async_copy(steps_in, steps, step_sem)
    asked.start()
    if not alone:
        asked.wait()
        needed = [
            functools.reduce(jnp.logical_or, [steps[k] == owner for k in range(count)])
            for owner in owners
        ]

    def departure(b, k, c):
        return pltpu.make_async_copy(
            done.at[b, pl.ds(c * part, part)],
            out.at[k, pl.ds(offset + c * part, part)],
            out_sem.at[b, k, c],
        )

    def compute(b, owner):
        for s in range(sources):
            parts = (near[b][s], far[b][s])
            turned[s // GROUP, s % GROUP] = jnp.concatenate(parts * per_tile).T
        for m in range(bins // span):
            at = m * span
            sums = []
            for p in range(GROUP):
                mine = turned[:, p, at : at + span, :]
                wide = jnp.concatenate(
                    [
                        jnp.where(
                            (row == q * per_tile + col)[None], mine, jnp.zeros_like(mine)
                        ).reshape(sources * GROUP, 128)
                        for q in range(tiles)
                    ],
                    axis=1,
                )
                start = (GROUP * m + p) * depth
                x = jnp.dot(
                    wide, weights[start : start + depth, :], preferred_element_type=jnp.float32
                )
                sums.append(x.reshape(sources // 2, 2 * GROUP, 2 * receivers))
            eights = []
            for p in range(0, GROUP, 2):
                low, high = sums[p], sums[p + 1]
                upper = lax.broadcasted_iota(jnp.int32, low.shape, 1) < GROUP
                one = jnp.where(upper, low, pltpu.roll(high, GROUP, 1))
                two = jnp.where(upper, pltpu.roll(low, GROUP, 1), high)
                eights.append(
                    jnp.stack((one, two), axis=1).reshape(sources, 2 * GROUP, 2 * receivers)
                )
            cross[:, at : at + span, :] = jnp.concatenate(eights, axis=1).astype(jnp.bfloat16)
        if alone:
            asked.wait()
        for c in range(parts_out):
            turns = [cross[c * part + i].T for i in range(part)]
            left = jnp.concatenate(
                [jnp.concatenate([x[:receivers], x[receivers:]], axis=1) for x in turns]
            )
            y = jnp.dot(left, table[...], preferred_element_type=jnp.float32)
            done[b, c * part : (c + 1) * part] = y.reshape(part, receivers, LAGS).astype(
                jnp.bfloat16
            )
            for k in range(count):
                @pl.when(steps[k] == owner)
                def _(k=k, c=c):
                    departure(b, k, c).start()

    for b in range(blocks):
        if alone:
            compute(b, owners[b])
        else:
            pl.when(needed[b])(functools.partial(compute, b, owners[b]))
    for b in range(blocks):
        for k in range(count):
            @pl.when(steps[k] == owners[b])
            def _(b=b, k=k):
                for c in range(parts_out):
                    departure(b, k, c).wait()


def stack(distances, tour, steps, table, weights, pieces, previous, out_shape, offset=0):
    blocks = len(distances)
    first = previous is None
    sources, rows, bins = pieces[0].shape
    receivers = weights.shape[1] // 2
    count = steps.shape[0]
    args = [steps, table, weights, *pieces] + ([] if first else [previous])
    return pl.pallas_call(
        functools.partial(stack_kernel, tour, distances, first, offset),
        out_shape=out_shape,
        in_specs=[pl.BlockSpec(memory_space=pl.ANY)]
        + [pl.BlockSpec(memory_space=VMEM)] * (2 + len(pieces))
        + [pl.BlockSpec(memory_space=pl.ANY)] * (0 if first else 1),
        out_specs=pl.BlockSpec(memory_space=pl.ANY),
        scratch_shapes=[
            SMEM(steps.shape, steps.dtype),
            VMEM((sources // GROUP, GROUP, bins, 128), jnp.bfloat16),
            VMEM((sources, bins, 2 * receivers), jnp.bfloat16),
            VMEM((blocks, sources, receivers, LAGS), jnp.bfloat16),
            pltpu.SemaphoreType.DMA((blocks, count, 2)),
            pltpu.SemaphoreType.DMA,
        ],
        input_output_aliases={} if first else {len(args) - 1: 0},
        compiler_params=pltpu.CompilerParams(vmem_limit_bytes=24 << 20),
        cost_estimate=SMALL,
        name="stack",
    )(*args)


def shards(ring, spectra, channel_mask, window_mask, source_block):
    count = len(ring)
    channels, windows, parts, bins = spectra.shape
    steps = source_block.shape[0]
    halves = lax.axis_size("tm")
    rows = spectra.reshape(channels, windows * parts, bins)
    same, other, both = whiten(rows, channel_mask, window_mask)

    def send(x, direction, cross=False):
        pairs = []
        for i in range(count):
            a, b = ring[i], ring[(i + direction) % count]
            for t in range(2):
                pairs.append((2 * a + t, 2 * b + (1 - t if cross else t)))
        return lax.ppermute(x, ("chan", "tm"), pairs)

    table = lag_tables(windows * halves, bins)

    half = count // 2
    early = [send(same, 1), send(other, -1, True)]
    far = lax.ppermute(both, "tm", [(0, 1), (1, 0)])
    late = [send(other, 1, True), send(same, -1)]
    weights = receiver_weights(both, far)
    run = functools.partial(
        stack,
        out_shape=jax.ShapeDtypeStruct((steps, channels // 2, channels, LAGS), jnp.bfloat16),
    )
    rest = (tuple(ring), source_block, table)

    def tie(pieces, token):
        tied = []
        for piece in pieces:
            piece, token = lax.optimization_barrier((piece, token))
            tied.append(piece)
        return tied, token

    out = None
    held = []
    for hop in range(1, half):
        closing = hop == half - 1
        if hop == 1:
            early, weights = tie(early, weights)
        else:
            early, out = tie(early, out)
        shares = 2 if closing else 1
        share = channels // 2 // shares
        coming = [
            [send(piece[i * share : (i + 1) * share], way) for piece, way in zip(early, (1, -1))]
            for i in range(shares)
        ]
        if hop == 1:
            late, weights = tie(late, weights)
        held.append((early[0], late[0], late[1], early[1]))
        if hop == 1:
            out = run((0,), *rest, weights, (same, far), None)
        elif not closing:
            out = run((1 - hop, hop - 1), *rest, weights, held[hop - 2], out)
            late, out = tie(late, out)
        if not closing:
            later = [send(late[0], 1), send(late[1], -1)]
        if 1 < hop == half - 2:
            out = run((-hop, hop), *rest, weights, held[hop - 1], out)
        if not closing:
            (early,), late = coming, later
    hop = half - 1
    out = run((-hop, hop), *rest, weights, held[hop - 1], out)
    for i, pieces in enumerate(coming):
        out = run((half,), *rest, weights, pieces, out, offset=i * share)
    return out


def solution(mesh):
    placed = (P(("grp", "chan"), "tm", None, None), P(("grp", "chan")), P(("grp", "tm")), P())
    return jax.shard_map(
        functools.partial(shards, ring_order(mesh)),
        mesh=mesh,
        in_specs=placed,
        out_specs=P(None, "tm", ("grp", "chan"), None),
        check_vma=False,
    )
```

```python
import functools
import math

import jax
import jax.numpy as jnp
import numpy as np
from jax import lax
from jax.experimental import pallas as pl
from jax.experimental.pallas import tpu as pltpu
from jax.sharding import PartitionSpec as P

LAGS = 128
NFFT = 8192
LOW_BIN = 8
LAG_STEP = 28
WATER = 0.1
BATCH = 8
GROUP = 4

VMEM = pltpu.VMEM
SMEM = pltpu.SMEM
SMALL = pl.CostEstimate(flops=1 << 20, bytes_accessed=1 << 14, transcendentals=0)


def ring_order(mesh):
    count = mesh.shape["chan"]
    natural = list(range(count))
    folded = natural[0::2] + natural[1::2][::-1]
    if count % 2:
        return natural
    grid = np.moveaxis(mesh.devices, mesh.axis_names.index("chan"), 0).reshape(count, -1)[:, 0]
    places = [getattr(device, "coords", None) for device in grid]
    if any(place is None for place in places):
        return folded if count == 8 else natural

    def length(tour):
        return sum(
            sum(abs(a - b) for a, b in zip(places[tour[i]], places[tour[i - 1]]))
            for i in range(count)
        )

    return folded if length(folded) < length(natural) else natural


def lag_tables(windows, bins):
    freq = np.arange(bins) + LOW_BIN
    lag = (np.arange(LAGS) - LAGS // 2) * LAG_STEP
    phase = (freq[:, None] * lag[None, :] % NFFT) * (2.0 * math.pi / NFFT)
    table = np.concatenate((np.cos(phase), -np.sin(phase))) / math.sqrt(windows * bins)
    return jnp.asarray(table, jnp.float32).astype(jnp.bfloat16)


def exchange(first, second, size):
    bins = first.shape[-1]
    lane = lax.broadcasted_iota(jnp.int32, first.shape, 1)
    even = lane // size % 2 == 0
    return (
        jnp.where(even, first, pltpu.roll(second, size, 1)),
        jnp.where(even, pltpu.roll(first, bins - size, 1), second),
    )


def interleave(a, b, c, d):
    a, c = exchange(a, c, 2 * GROUP)
    b, d = exchange(b, d, 2 * GROUP)
    return exchange(a, b, GROUP) + exchange(c, d, GROUP)


def whiten_kernel(chan_in, win_in, spectra, same, other, both, held, chan_mask, win_mask, sems):
    rows, bins = spectra.shape[1:]
    half = same.shape[0]
    own = lax.axis_index("tm") * half
    starts = (own, half - own)
    copies = [
        pltpu.make_async_copy(spectra.at[pl.ds(start, half)], held.at[i], sems.at[i])
        for i, start in enumerate(starts)
    ]
    masks = [
        pltpu.make_async_copy(win_in, win_mask, sems.at[2]),
        pltpu.make_async_copy(chan_in, chan_mask, sems.at[3]),
    ]
    for copy in copies + masks:
        copy.start()
    for copy in masks:
        copy.wait()
    row = lax.broadcasted_iota(jnp.int32, (rows, bins), 0)
    keep = jnp.zeros((rows, bins), jnp.float32)
    for w in range(rows // 2):
        keep = jnp.where(row // 2 == w, win_mask[w].astype(jnp.float32), keep)

    source = lax.broadcasted_iota(jnp.int32, (bins, bins), 0)
    target = lax.broadcasted_iota(jnp.int32, (bins, bins), 1)
    band = sum(
        jnp.where(source == jnp.clip(target + d, 0, bins - 1), 1.0, 0.0) for d in range(-2, 3)
    ).astype(jnp.bfloat16)
    band = jnp.concatenate([band] * 3)

    def with_partner(square):
        even = lax.broadcasted_iota(jnp.int32, square.shape, 0) % 2 == 0
        last = square.shape[0] - 1
        return square + jnp.where(even, pltpu.roll(square, last, 0), pltpu.roll(square, 1, 0))

    def whitened(side, channels):
        values = jnp.concatenate([held[side, c].astype(jnp.float32) for c in channels])
        square = values * values
        power = jnp.concatenate(
            [with_partner(square[i : i + 8]) for i in range(0, square.shape[0], 8)]
        )
        magnitude = jnp.sqrt(power)
        high = magnitude.astype(jnp.bfloat16)
        rest = magnitude - high.astype(jnp.float32)
        middle = rest.astype(jnp.bfloat16)
        low = (rest - middle.astype(jnp.float32)).astype(jnp.bfloat16)
        smoothed = (
            jnp.dot(
                jnp.concatenate((high, middle, low), axis=1),
                band,
                preferred_element_type=jnp.float32,
            )
            / 5.0
        )
        kept = jnp.concatenate([keep * chan_mask[starts[side] + c].astype(jnp.float32) for c in channels])
        return values * (kept / (smoothed + WATER))

    for side, piece in enumerate((same, other)):
        copies[side].wait()
        for i in range(0, half, BATCH):
            values = whitened(side, range(i, i + BATCH))
            for j in range(0, BATCH, GROUP):
                mixed = interleave(
                    *(values[n * rows : (n + 1) * rows] for n in range(j, j + GROUP))
                )
                for n, one in enumerate(mixed):
                    one = one.astype(jnp.bfloat16)
                    piece[i + j + n] = one
                    both[side * half + i + j + n] = one


def whiten(spectra, chan_mask, win_mask):
    channels, rows, bins = spectra.shape
    piece = VMEM((channels // 2, rows, bins), jnp.bfloat16)
    return pl.pallas_call(
        whiten_kernel,
        out_shape=(piece, piece, VMEM((channels, rows, bins), jnp.bfloat16)),
        in_specs=[pl.BlockSpec(memory_space=pl.ANY)] * 3,
        out_specs=(pl.BlockSpec(memory_space=VMEM),) * 3,
        scratch_shapes=[
            VMEM((2, channels // 2, rows, bins), jnp.bfloat16),
            SMEM(chan_mask.shape, chan_mask.dtype),
            SMEM(win_mask.shape, win_mask.dtype),
            pltpu.SemaphoreType.DMA((4,)),
        ],
        cost_estimate=SMALL,
        name="whiten",
    )(chan_mask, win_mask, spectra)


def receiver_kernel(both, far, weights, flat, wide, held, sems):
    half, rows, bins = held.shape[1:]
    copies = [
        pltpu.make_async_copy(piece.at[pl.ds(start, half)], held.at[i], sems.at[i])
        for i, (piece, start) in enumerate(((both, 0), (far, half), (both, half), (far, 0)))
    ]
    for copy in copies:
        copy.start()
    mine = lax.axis_index("tm") * half
    theirs = half - mine
    deep = 2 * rows
    for side, start in enumerate((mine, theirs)):
        for h in range(2):
            copies[2 * side + h].wait()
            piece = held.at[2 * side + h]
            for i in range(0, half, GROUP):
                apart = interleave(*(piece[i + j].astype(jnp.float32) for j in range(GROUP)))
                for j, one in enumerate(apart):
                    at = pl.multiple_of((start + i + j) * deep + h * rows, rows)
                    flat[pl.ds(at, rows), :] = one
    for w in range(rows):
        real = flat[pl.ds(2 * w, 2 * half, stride=deep), :]
        imag = flat[pl.ds(2 * w + 1, 2 * half, stride=deep), :]
        wide[pl.ds(2 * w, bins, stride=deep), :] = jnp.concatenate((real, imag)).T
        wide[pl.ds(2 * w + 1, bins, stride=deep), :] = jnp.concatenate((imag, -real)).T
    weights[...] = wide[...].astype(jnp.bfloat16)


def receiver_weights(both, far):
    channels, rows, bins = both.shape
    half = channels // 2
    return pl.pallas_call(
        receiver_kernel,
        out_shape=jax.ShapeDtypeStruct((bins * 2 * rows, 4 * half), jnp.bfloat16),
        in_specs=[pl.BlockSpec(memory_space=pl.ANY)] * 2,
        out_specs=pl.BlockSpec(memory_space=VMEM),
        scratch_shapes=[
            VMEM((2 * half * 2 * rows, bins), jnp.float32),
            VMEM((bins * 2 * rows, 4 * half), jnp.float32),
            VMEM((4, half, rows, bins), jnp.bfloat16),
            pltpu.SemaphoreType.DMA((4,)),
        ],
        compiler_params=pltpu.CompilerParams(vmem_limit_bytes=24 << 20),
        cost_estimate=SMALL,
        name="receiver_weights",
    )(both, far)


def stack_kernel(tour, distances, first, offset, steps_in, table, weights, *refs):
    blocks = len(distances)
    pieces = refs[: 2 * blocks]
    out = refs[2 * blocks + (0 if first else 1)]
    steps, turned, cross, done, out_sem, step_sem = refs[2 * blocks + (1 if first else 2) :]
    sources, receivers, _ = done.shape[1:]
    rows, bins = pieces[0].shape[1:]
    count = steps.shape[0]
    ring = len(tour)
    alone = blocks == 1 and not first
    lanes = 2 * rows
    per_tile = 128 // lanes
    tiles = GROUP // per_tile
    depth = GROUP * lanes
    span = GROUP * GROUP
    row = lax.broadcasted_iota(jnp.int32, (span, 128), 0) % GROUP
    col = lax.broadcasted_iota(jnp.int32, (span, 128), 1) // lanes
    near = pieces[0::2]
    far = [piece.at[pl.ds(sources, sources)] if first else piece for piece in pieces[1::2]]
    me = lax.axis_index("chan")
    folded = tour[1] == 2

    def owner_at(distance):
        at = jnp.where(me % 2 == 0, me // 2, ring - 1 - me // 2) if folded else me
        at = lax.rem(at + distance + ring, ring)
        return jnp.where(at < ring // 2, 2 * at, 2 * (ring - 1 - at) + 1) if folded else at

    owners = [owner_at(d) for d in distances]
    parts_out = out_sem.shape[2]
    part = sources // parts_out
    asked = pltpu.make_async_copy(steps_in, steps, step_sem)
    asked.start()
    if not alone:
        asked.wait()
        needed = [
            functools.reduce(jnp.logical_or, [steps[k] == owner for k in range(count)])
            for owner in owners
        ]

    def departure(b, k, c):
        return pltpu.make_async_copy(
            done.at[b, pl.ds(c * part, part)],
            out.at[k, pl.ds(offset + c * part, part)],
            out_sem.at[b, k, c],
        )

    def compute(b, owner):
        for s in range(sources):
            parts = (near[b][s], far[b][s])
            turned[s // GROUP, s % GROUP] = jnp.concatenate(parts * per_tile).T
        for m in range(bins // span):
            at = m * span
            sums = []
            for p in range(GROUP):
                mine = turned[:, p, at : at + span, :]
                wide = jnp.concatenate(
                    [
                        jnp.where(
                            (row == q * per_tile + col)[None], mine, jnp.zeros_like(mine)
                        ).reshape(sources * GROUP, 128)
                        for q in range(tiles)
                    ],
                    axis=1,
                )
                start = (GROUP * m + p) * depth
                x = jnp.dot(
                    wide, weights[start : start + depth, :], preferred_element_type=jnp.float32
                )
                sums.append(x.reshape(sources // 2, 2 * GROUP, 2 * receivers))
            eights = []
            for p in range(0, GROUP, 2):
                low, high = sums[p], sums[p + 1]
                upper = lax.broadcasted_iota(jnp.int32, low.shape, 1) < GROUP
                one = jnp.where(upper, low, pltpu.roll(high, GROUP, 1))
                two = jnp.where(upper, pltpu.roll(low, GROUP, 1), high)
                eights.append(
                    jnp.stack((one, two), axis=1).reshape(sources, 2 * GROUP, 2 * receivers)
                )
            cross[:, at : at + span, :] = jnp.concatenate(eights, axis=1).astype(jnp.bfloat16)
        if alone:
            asked.wait()
        for c in range(parts_out):
            turns = [cross[c * part + i].T for i in range(part)]
            left = jnp.concatenate(
                [jnp.concatenate([x[:receivers], x[receivers:]], axis=1) for x in turns]
            )
            y = jnp.dot(left, table[...], preferred_element_type=jnp.float32)
            done[b, c * part : (c + 1) * part] = y.reshape(part, receivers, LAGS).astype(
                jnp.bfloat16
            )
            for k in range(count):
                @pl.when(steps[k] == owner)
                def _(k=k, c=c):
                    departure(b, k, c).start()

    for b in range(blocks):
        if alone:
            compute(b, owners[b])
        else:
            pl.when(needed[b])(functools.partial(compute, b, owners[b]))
    for b in range(blocks):
        for k in range(count):
            @pl.when(steps[k] == owners[b])
            def _(b=b, k=k):
                for c in range(parts_out):
                    departure(b, k, c).wait()


def stack(distances, tour, steps, table, weights, pieces, previous, out_shape, offset=0):
    blocks = len(distances)
    first = previous is None
    sources, rows, bins = pieces[0].shape
    receivers = weights.shape[1] // 2
    count = steps.shape[0]
    args = [steps, table, weights, *pieces] + ([] if first else [previous])
    return pl.pallas_call(
        functools.partial(stack_kernel, tour, distances, first, offset),
        out_shape=out_shape,
        in_specs=[pl.BlockSpec(memory_space=pl.ANY)]
        + [pl.BlockSpec(memory_space=VMEM)] * (2 + len(pieces))
        + [pl.BlockSpec(memory_space=pl.ANY)] * (0 if first else 1),
        out_specs=pl.BlockSpec(memory_space=pl.ANY),
        scratch_shapes=[
            SMEM(steps.shape, steps.dtype),
            VMEM((sources // GROUP, GROUP, bins, 128), jnp.bfloat16),
            VMEM((sources, bins, 2 * receivers), jnp.bfloat16),
            VMEM((blocks, sources, receivers, LAGS), jnp.bfloat16),
            pltpu.SemaphoreType.DMA((blocks, count, 1)),
            pltpu.SemaphoreType.DMA,
        ],
        input_output_aliases={} if first else {len(args) - 1: 0},
        compiler_params=pltpu.CompilerParams(vmem_limit_bytes=24 << 20),
        cost_estimate=SMALL,
        name="stack",
    )(*args)


def shards(ring, spectra, channel_mask, window_mask, source_block):
    count = len(ring)
    channels, windows, parts, bins = spectra.shape
    steps = source_block.shape[0]
    halves = lax.axis_size("tm")
    rows = spectra.reshape(channels, windows * parts, bins)
    same, other, both = whiten(rows, channel_mask, window_mask)

    def send(x, direction, cross=False):
        pairs = []
        for i in range(count):
            a, b = ring[i], ring[(i + direction) % count]
            for t in range(2):
                pairs.append((2 * a + t, 2 * b + (1 - t if cross else t)))
        return lax.ppermute(x, ("chan", "tm"), pairs)

    table = lag_tables(windows * halves, bins)

    half = count // 2
    early = [send(same, 1), send(other, -1, True)]
    far = lax.ppermute(both, "tm", [(0, 1), (1, 0)])
    late = [send(other, 1, True), send(same, -1)]
    weights = receiver_weights(both, far)
    run = functools.partial(
        stack,
        out_shape=jax.ShapeDtypeStruct((steps, channels // 2, channels, LAGS), jnp.bfloat16),
    )
    rest = (tuple(ring), source_block, table)

    def tie(pieces, token):
        tied = []
        for piece in pieces:
            piece, token = lax.optimization_barrier((piece, token))
            tied.append(piece)
        return tied, token

    out = None
    held = []
    for hop in range(1, half):
        closing = hop == half - 1
        if hop == 1:
            early, weights = tie(early, weights)
        else:
            early, out = tie(early, out)
        shares = 2 if closing else 1
        share = channels // 2 // shares
        coming = [
            [send(piece[i * share : (i + 1) * share], way) for piece, way in zip(early, (1, -1))]
            for i in range(shares)
        ]
        if hop == 1:
            late, weights = tie(late, weights)
        held.append((early[0], late[0], late[1], early[1]))
        if hop == 1:
            out = run((0,), *rest, weights, (same, far), None)
        elif not closing:
            out = run((1 - hop, hop - 1), *rest, weights, held[hop - 2], out)
            late, out = tie(late, out)
        if not closing:
            later = [send(late[0], 1), send(late[1], -1)]
        if 1 < hop == half - 2:
            out = run((-hop, hop), *rest, weights, held[hop - 1], out)
        if not closing:
            (early,), late = coming, later
    hop = half - 1
    out = run((-hop, hop), *rest, weights, held[hop - 1], out)
    for i, pieces in enumerate(coming):
        out = run((half,), *rest, weights, pieces, out, offset=i * share)
    return out


def solution(mesh):
    placed = (P(("grp", "chan"), "tm", None, None), P(("grp", "chan")), P(("grp", "tm")), P())
    return jax.shard_map(
        functools.partial(shards, ring_order(mesh)),
        mesh=mesh,
        in_specs=placed,
        out_specs=P(None, "tm", ("grp", "chan"), None),
        check_vma=False,
    )
```
